256 devices in a mesh: beam: 4 (over x_hi, core), row: 64 (over z, x_lo, y).
Axes of the slice: x: 4 (x_hi: 2, x_lo: 2; x = x_hi * 2 + x_lo), y: 4, z: 8, core: 2. Of those that a mesh axis runs over, the one named last changes fastest.
Arguments:
- field_in: bfloat16 [2, 1024, 32, 1024], P(None, 'row', 'beam'), may hold values from -6 to 6
- target: bfloat16 [2, 1024, 32, 1024], P(None, 'row', 'beam'), may hold values from -6 to 6
- phase: float32 [1024, 1024], P('row', 'beam'), may hold values from -3.1416 to 3.1416
- moment: float32 [1024, 1024], P('row', 'beam'), may hold values from -0.6 to 0.6
- second: float32 [1024, 1024], P('row', 'beam'), may hold values from 0.0001 to 0.001
Outputs:
- forward_out: bfloat16 [2, 1024, 32, 1024], P(None, 'row', 'beam')
- backward_out: bfloat16 [2, 1024, 32, 1024], P(None, 'row', 'beam')
- intersection: float32 [2, 32], P(None, 'beam')
- new_phase: float32 [1024, 1024], P('row', 'beam')
- new_moment: float32 [1024, 1024], P('row', 'beam')
- new_second: float32 [1024, 1024], P('row', 'beam')
The draws below stay inside these ranges and needn't reach their ends.
All inputs are finite; a program needn't handle non-finite values.
Results may differ from the reference program's by a relative error of at most 0.011.
Values may be sent and summed in bfloat16 or wider, within the bound.
No kernel may reach another device: no remote copies, remote signals or barrier semaphores. Data moves between devices by JAX's collectives and lax.ppermute only.
A program may use at most 128 MiB of HBM per device.

```python
import math
import jax
import jax.numpy as jnp
from jax import lax

N = 1024
STEP = 10
BEAMS = 32


def nyquist_tones(key, scale):
    row_index = jnp.arange(N, dtype=jnp.int32)
    summed = jnp.zeros((2, N, BEAMS, N), jnp.float32)
    for offset in range(4):
        key, amp_key, start_key = jax.random.split(key, 3)
        amplitude = jax.random.normal(amp_key, (2, 1, BEAMS, N), jnp.float32) * scale
        starting = jax.random.uniform(start_key, (2, 1, BEAMS, N), jnp.float32, -math.pi, math.pi)
        cycles = (N // 2 + offset) * row_index % N
        row_angle = cycles.astype(jnp.float32) * (2.0 * math.pi / N)
        summed = summed + amplitude * jnp.cos(row_angle[None, :, None, None] + starting)
    return summed


def draw_field_in(key, part):
    key = jax.random.fold_in(key, 11)
    tone_key, noise_key = jax.random.split(key)
    full_shape = (2, N, BEAMS, N)
    smooth_part = nyquist_tones(tone_key, 0.6)
    rough_part = jax.random.normal(noise_key, full_shape, jnp.float32) * 0.5
    return jnp.clip(smooth_part + rough_part, -6.0, 6.0).astype(jnp.bfloat16)


def draw_target(key, part):
    key = jax.random.fold_in(key, 23)
    tone_key, noise_key = jax.random.split(key)
    full_shape = (2, N, BEAMS, N)
    smooth_part = nyquist_tones(tone_key, 0.6)
    rough_part = jax.random.normal(noise_key, full_shape, jnp.float32) * 0.5
    return jnp.clip(smooth_part + rough_part, -6.0, 6.0).astype(jnp.bfloat16)


def draw_phase(key, part):
    key = jax.random.fold_in(key, 37)
    centre_key, depth_key, start_key, rough_key = jax.random.split(key, 4)
    centre = jax.random.uniform(centre_key, (1, N), jnp.float32, -2.2, 2.2)
    depth = jax.random.uniform(depth_key, (1, N), jnp.float32, 0.2, 0.7)
    starting = jax.random.uniform(start_key, (1, N), jnp.float32, -math.pi, math.pi)
    row_angle = jnp.arange(N, dtype=jnp.int32).astype(jnp.float32) * (2.0 * math.pi / N)
    rough_part = jax.random.uniform(rough_key, (N, N), jnp.float32, -0.2, 0.2)
    return centre + depth * jnp.sin(row_angle[:, None] + starting) + rough_part


def steps_of(key, extent, cuts, low, high):
    gain, own = 1.0, jax.random.fold_in(key, 6)
    for position, blocks in cuts:
        steps = jnp.exp(jax.random.uniform(jax.random.fold_in(own, position), (blocks,), jnp.float32, low / len(cuts), high / len(cuts)))
        gain = gain * jnp.repeat(steps, extent[position] // blocks).reshape([-1 if axis == position else 1 for axis in range(len(extent))])
    return gain


def normal_values(rng, shape, deviation, most, pieces=(), held_as=jnp.bfloat16):
    array = deviation * jax.random.normal(rng, shape, jnp.float32)
    if pieces:
        array = array * steps_of(rng, shape, pieces, -0.22, 0.18)
    return jnp.clip(array, -most, most).astype(held_as)


def setup_inputs(seed: int = 0) -> dict:
    splits = jax.random.split(jax.random.key(seed), 6)
    field_in = draw_field_in(jax.random.fold_in(splits[5], 71), 0)
    target = draw_target(jax.random.fold_in(splits[5], 71), 0)
    phase = draw_phase(jax.random.fold_in(splits[5], 71), 0)
    moment = normal_values(splits[3], (N, N), 0.15, 0.6, ((0, 64), (1, 4)), jnp.float32)
    second = jnp.clip(jnp.exp(math.log(0.001) - 2.3025852 * jax.random.uniform(splits[4], (N, N), jnp.float32) ** steps_of(splits[4], (N, N), ((0, 64), (1, 4)), -0.2, 0.2)), 0.0001, 0.001)
    return {"field_in": field_in, "target": target, "phase": phase, "moment": moment, "second": second}


learn_rate = 0.4

def tables():
    index = jnp.arange(N, dtype=jnp.int32)
    product = index[:, None] * index[None, :] % N
    angle = product.astype(jnp.float32) * (2.0 * math.pi / N)
    scale = 1.0 / math.sqrt(N)
    return ((jnp.cos(angle) * scale).astype(jnp.bfloat16), (jnp.sin(angle) * scale).astype(jnp.bfloat16))

def transfer():
    index = jnp.arange(N, dtype=jnp.int32)
    freq = jnp.where(index < N // 2, index, index - N).astype(jnp.float32)
    half = float(N // 2)
    rho = (freq[:, None] ** 2 + freq[None, :] ** 2) / (half * half)
    theta = -60.0 * rho / (1.0 + jnp.sqrt(1.0 - 0.4 * rho))
    return (jnp.cos(theta), jnp.sin(theta))

def mm(a, b):
    return jnp.dot(a, b, preferred_element_type=jnp.float32)

def propagate(xr, xi, ctab, stab, hc, hs):
    ar = (mm(xr, ctab) + mm(xi, stab)).astype(jnp.bfloat16)
    ai = (mm(xi, ctab) - mm(xr, stab)).astype(jnp.bfloat16)
    br = mm(ctab, ar) + mm(stab, ai)
    bi = mm(ctab, ai) - mm(stab, ar)
    cr = (br * hc - bi * hs).astype(jnp.bfloat16)
    ci = (br * hs + bi * hc).astype(jnp.bfloat16)
    dr = (mm(ctab, cr) - mm(stab, ci)).astype(jnp.bfloat16)
    di = (mm(ctab, ci) + mm(stab, cr)).astype(jnp.bfloat16)
    return (mm(dr, ctab) - mm(di, stab), mm(di, ctab) + mm(dr, stab))

def reference(field_in, target, phase, moment, second):
    ctab, stab = tables()
    hc, hs = transfer()
    cosp = jnp.cos(phase)
    sinp = jnp.sin(phase)
    fields = jnp.moveaxis(field_in, 2, 0)
    targets = jnp.moveaxis(target, 2, 0)

    def one_beam(carry, pair):
        field, goal = pair
        ur = field[0].astype(jnp.float32)
        ui = field[1].astype(jnp.float32)
        wr = ur * cosp - ui * sinp
        wi = ur * sinp + ui * cosp
        fr, fi = propagate(wr.astype(jnp.bfloat16), wi.astype(jnp.bfloat16), ctab, stab, hc, hs)
        ar, ai = propagate(goal[0], goal[1], ctab, stab, hc, -hs)
        tr = goal[0].astype(jnp.float32)
        ti = goal[1].astype(jnp.float32)
        ore = jnp.sum(tr * fr + ti * fi) / N
        oim = jnp.sum(tr * fi - ti * fr) / N
        zr = ar * wr + ai * wi
        zi = ar * wi - ai * wr
        carry = carry + (ore * zi - oim * zr)
        back_r = ar * cosp + ai * sinp
        back_i = ai * cosp - ar * sinp
        fwd = jnp.stack([fr, fi]).astype(jnp.bfloat16)
        back = jnp.stack([back_r, back_i]).astype(jnp.bfloat16)
        return (carry, (fwd, back, jnp.stack([ore, oim])))
    total, outs = lax.scan(one_beam, jnp.zeros((N, N), jnp.float32), (fields, targets))
    fwd_all, back_all, over_all = outs
    grad = -(2.0 / BEAMS) * total
    new_moment = 0.9 * moment + 0.1 * grad
    new_second = 0.999 * second + 0.001 * grad * grad
    corr_one = 1.0 - 0.9 ** STEP
    corr_two = 1.0 - 0.999 ** STEP
    new_phase = phase - learn_rate * (new_moment / corr_one) / (jnp.sqrt(new_second / corr_two) + 1e-08)
    return (jnp.moveaxis(fwd_all, 0, 2), jnp.moveaxis(back_all, 0, 2), jnp.transpose(over_all), new_phase, new_moment, new_second)
```

```python
import functools
import math

import jax
import jax.numpy as jnp
import ml_dtypes
import numpy as np
from jax import lax
from jax.experimental import pallas as pl
from jax.experimental.pallas import tpu as pltpu
from jax.sharding import PartitionSpec as P


STEP = 10
N = 1024
BEAMS = 32
learn_rate = 0.4
f32 = jnp.float32
bf16 = jnp.bfloat16
VMEM_LIMIT = 48 * 1024 * 1024


def angles(product, size):
    turn = (product % size) * (2.0 * math.pi / size)
    return np.cos(turn), np.sin(turn)


def as_bf16(array):
    return array.astype(np.float32).astype(ml_dtypes.bfloat16)


@functools.lru_cache(None)
def host_tables():
    k = np.arange(256)
    col_left, col_right = [], []
    for rho in range(4):
        c, s = angles((4 * k[:, None] + rho) * k[None, :], 1024)
        col_left.append(np.concatenate([c, s], 0) / 32.0)
        col_right.append(np.concatenate([c, s], 1) / 32.0)
    q = np.arange(16)
    row_in, row_out = [], []
    eye = np.eye(16)
    for sigma in range(4):
        c, s = angles((4 * q[:, None] + sigma) * q[None, :], 64)
        row_in.append(np.concatenate([np.kron(c, eye), np.kron(s, eye)], 0) / 8.0)
        row_out.append(np.concatenate([np.kron(c.T, eye), np.kron(s.T, eye)], 0) / 8.0)
    c, s = angles(q[:, None] * q[None, :], 16)
    kc, ks = np.kron(c, np.eye(8)) / 4.0, np.kron(s, np.eye(8)) / 4.0
    lane_in = np.block([[kc, -ks], [ks, kc]])
    lane_out = np.block([[kc, ks], [-ks, kc]])
    k1 = 4 * q[None, :, None] + np.arange(4)[:, None, None]
    r = np.repeat(q, 8)[None, None, :]
    twist = np.stack(angles(k1 * r, 1024)).astype(np.float32)
    return dict(
        col_left=as_bf16(np.stack(col_left)),
        col_right=as_bf16(np.stack(col_right)),
        row_in=as_bf16(np.stack(row_in)),
        row_out=as_bf16(np.stack(row_out)),
        lane_in=as_bf16(lane_in),
        lane_out=as_bf16(lane_out),
        twist=twist,
    )


def frequency(index):
    return jnp.where(index < N // 2, index, index - N).astype(f32)


def transfer(row_index):
    rho, a = row_index // 16, row_index % 16
    shape = (4, 16, 16, 128)
    sigma = lax.broadcasted_iota(jnp.int32, shape, 0)
    q = lax.broadcasted_iota(jnp.int32, shape, 1)
    t = lax.broadcasted_iota(jnp.int32, shape, 2)
    k2 = lax.broadcasted_iota(jnp.int32, shape, 3) // 8
    fy = frequency(4 * q + sigma + 64 * k2)
    fx = frequency(4 * (16 * a + t) + rho)
    half = float(N // 2)
    rad = (fy**2 + fx**2) / (half * half)
    theta = -60.0 * rad / (1.0 + jnp.sqrt(1.0 - 0.4 * rad))
    return jnp.stack([jnp.cos(theta), jnp.sin(theta)]).reshape(2, 4, 256, 128)


def split_four(x):
    e0 = [x[0][p] + x[2][p] for p in (0, 1)]
    e1 = [x[0][p] - x[2][p] for p in (0, 1)]
    o0 = [x[1][p] + x[3][p] for p in (0, 1)]
    o1 = [x[1][p] - x[3][p] for p in (0, 1)]
    return (
        (e0[0] + o0[0], e0[1] + o0[1]),
        (e1[0] + o1[1], e1[1] - o1[0]),
        (e0[0] - o0[0], e0[1] - o0[1]),
        (e1[0] - o1[1], e1[1] + o1[0]),
    )


def join_four(x):
    e0 = [x[0][p] + x[2][p] for p in (0, 1)]
    e1 = [x[0][p] - x[2][p] for p in (0, 1)]
    o0 = [x[1][p] + x[3][p] for p in (0, 1)]
    o1 = [x[1][p] - x[3][p] for p in (0, 1)]
    return (
        (e0[0] + o0[0], e0[1] + o0[1]),
        (e1[0] - o1[1], e1[1] + o1[0]),
        (e0[0] - o0[0], e0[1] - o0[1]),
        (e1[0] + o1[1], e1[1] - o1[0]),
    )


def dot(a, b, dims=((1,), (0,))):
    return lax.dot_general(a, b, (dims, ((), ())), preferred_element_type=f32)


def over_beams(rows):
    return jnp.broadcast_to(rows[:, None, :], (16, 8, rows.shape[1])).reshape(128, rows.shape[1])


def cols_in(parts, table_ref, out_ref):
    for rho, (ur, ui) in enumerate(split_four(parts)):
        both = jnp.concatenate([ur.astype(bf16), ui.astype(bf16)], 0)
        prod = dot(table_ref[rho], both, ((1,), (1,)))
        yr = prod[:256, :128] + prod[256:, 128:]
        yi = prod[:256, 128:] - prod[256:, :128]
        out_ref[16 * rho : 16 * rho + 16, 0:16, :] = yr.astype(bf16).reshape(16, 16, 128)
        out_ref[16 * rho : 16 * rho + 16, 16:32, :] = yi.astype(bf16).reshape(16, 16, 128)


def target_in_kernel(x_ref, table_ref, out_ref):
    parts = []
    for m in range(4):
        cut = pl.ds(256 * m, 256)
        parts.append((x_ref[0, :, cut].astype(f32), x_ref[1, :, cut].astype(f32)))
    cols_in(parts, table_ref, out_ref)


def field_in_kernel(x_ref, phase_ref, table_ref, out_ref):
    parts = []
    for m in range(4):
        cut = pl.ds(256 * m, 256)
        ur, ui = x_ref[0, :, cut].astype(f32), x_ref[1, :, cut].astype(f32)
        phase = phase_ref[:, cut]
        c, s = over_beams(jnp.cos(phase)), over_beams(jnp.sin(phase))
        parts.append((ur * c - ui * s, ur * s + ui * c))
    cols_in(parts, table_ref, out_ref)


def rows_pass(v_ref, row_in, row_out, lane_in, lane_out, twist, h_ref, sign):
    parts = []
    for m in range(4):
        cut = pl.ds(16 * m, 16)
        parts.append(
            (
                v_ref[cut, 0:16, :].astype(f32).reshape(256, 128),
                v_ref[cut, 16:32, :].astype(f32).reshape(256, 128),
            )
        )
    done = []
    for sigma, (ur, ui) in enumerate(split_four(parts)):
        both = jnp.concatenate([ur.astype(bf16), ui.astype(bf16)], 1)
        prod = dot(row_in[sigma], both)
        ar = (prod[:256, :128] + prod[256:, 128:]).reshape(16, 16, 128)
        ai = (prod[:256, 128:] - prod[256:, :128]).reshape(16, 16, 128)
        tc, ts = twist[0, sigma][:, None, :], twist[1, sigma][:, None, :]
        br = (ar * tc + ai * ts).astype(bf16).reshape(256, 128)
        bi = (ai * tc - ar * ts).astype(bf16).reshape(256, 128)
        spec = dot(jnp.concatenate([br, bi], 1), lane_in[...])
        dr, di = spec[:, :128], spec[:, 128:]
        hc, hs = h_ref[0, sigma], h_ref[1, sigma]
        if sign > 0:
            er, ei = dr * hc - di * hs, dr * hs + di * hc
        else:
            er, ei = dr * hc + di * hs, di * hc - dr * hs
        both = jnp.concatenate([er.astype(bf16), ei.astype(bf16)], 1)
        back = dot(both, lane_out[...])
        gr, gi = back[:, :128].reshape(16, 16, 128), back[:, 128:].reshape(16, 16, 128)
        hr = (gr * tc - gi * ts).astype(bf16).reshape(256, 128)
        hi = (gi * tc + gr * ts).astype(bf16).reshape(256, 128)
        prod = dot(row_out[sigma], jnp.concatenate([hr, hi], 1))
        done.append(
            (prod[:256, :128] - prod[256:, 128:], prod[:256, 128:] + prod[256:, :128])
        )
    return join_four(done)


def target_rows_kernel(v_ref, row_in, row_out, lane_in, lane_out, twist, h_ref, out_ref):
    done = rows_pass(v_ref, row_in, row_out, lane_in, lane_out, twist, h_ref, -1)
    for m in range(4):
        for p in (0, 1):
            out_ref[16 * m : 16 * m + 16, 16 * p : 16 * p + 16, :] = (
                done[m][p].astype(bf16).reshape(16, 16, 128)
            )


def field_rows_kernel(v_ref, t_ref, row_in, row_out, lane_in, lane_out, twist, h_ref, out_ref):
    done = rows_pass(v_ref, row_in, row_out, lane_in, lane_out, twist, h_ref, 1)
    sum_re = jnp.zeros((8, 128), f32)
    sum_im = jnp.zeros((8, 128), f32)
    for m in range(4):
        cut = pl.ds(16 * m, 16)
        for p in (0, 1):
            out_ref[16 * m : 16 * m + 16, 16 * p : 16 * p + 16, :] = (
                done[m][p].astype(bf16).reshape(16, 16, 128)
            )
        fr, fi = done[m]
        tr = t_ref[cut, 0:16, :].astype(f32).reshape(256, 128)
        ti = t_ref[cut, 16:32, :].astype(f32).reshape(256, 128)
        sum_re = sum_re + jnp.sum((tr * fr + ti * fi).reshape(32, 8, 128), 0)
        sum_im = sum_im + jnp.sum((tr * fi - ti * fr).reshape(32, 8, 128), 0)
    re = jnp.sum(sum_re, 0, keepdims=True)
    im = jnp.sum(sum_im, 0, keepdims=True)
    re_hi, im_hi = re.astype(bf16).astype(f32), im.astype(bf16).astype(f32)
    tail = jnp.concatenate([re_hi, im_hi, re - re_hi, im - im_hi, jnp.zeros((4, 128), f32)], 0)
    out_ref[:, 32:40, :] = jnp.broadcast_to(tail.astype(bf16)[None], (64, 8, 128))


def cols_out(v_ref, table_ref):
    done = []
    for rho in range(4):
        cut = pl.ds(16 * rho, 16)
        both = jnp.concatenate(
            [v_ref[cut, 0:16, :].reshape(256, 128), v_ref[cut, 16:32, :].reshape(256, 128)], 1
        )
        prod = dot(both, table_ref[rho], ((0,), (0,)))
        done.append(
            (prod[:128, :256] - prod[128:, 256:], prod[128:, :256] + prod[:128, 256:])
        )
    return join_four(done)


def target_out_kernel(v_ref, x_ref, phase_ref, table_ref, back_ref, z_ref):
    for m, (ar, ai) in enumerate(cols_out(v_ref, table_ref)):
        cut = pl.ds(256 * m, 256)
        phase = phase_ref[:, cut]
        c, s = over_beams(jnp.cos(phase)), over_beams(jnp.sin(phase))
        br, bi = ar * c + ai * s, ai * c - ar * s
        back_ref[0, :, cut] = br.astype(bf16)
        back_ref[1, :, cut] = bi.astype(bf16)
        ur, ui = x_ref[0, :, cut].astype(f32), x_ref[1, :, cut].astype(f32)
        z_ref[0, :, cut] = br * ur + bi * ui
        z_ref[1, :, cut] = br * ui - bi * ur


def grad_kernel(v_ref, z_ref, over_ref, own_ref, one_ref, two_ref, three_ref, whole):
    rows = jnp.sum(v_ref[:, 32:40, :].astype(f32), 0)
    lane = lax.broadcasted_iota(jnp.int32, (8, 128), 1) % 8
    beam = lax.broadcasted_iota(jnp.int32, (8, 128), 0)
    sums = []
    for p in (0, 1):
        line = (rows[p : p + 1] + rows[p + 2 : p + 3]) / N
        picked = jnp.where(lane == beam, jnp.broadcast_to(line, (8, 128)), 0.0)
        sums.append(jnp.sum(picked, 1, keepdims=True))
    lanes = lax.broadcasted_iota(jnp.int32, (8, 8), 1)
    beams = lax.broadcasted_iota(jnp.int32, (8, 8), 0)
    for p in (0, 1):
        over_ref[p : p + 1, :] = jnp.sum(jnp.where(lanes == beams, sums[p], 0.0), 0, keepdims=True)
    for m in range(4):
        cut = pl.ds(256 * m, 256)
        zr = z_ref[0, :, cut].reshape(16, 8, 256)
        zi = z_ref[1, :, cut].reshape(16, 8, 256)
        whole[m] = -(2.0 / BEAMS) * jnp.sum(sums[0][None] * zi - sums[1][None] * zr, 1)
    me = lax.axis_index("beam")
    for step, ref in enumerate((own_ref, one_ref, two_ref, three_ref)):
        ref[...] = whole[me ^ step]


def field_out_kernel(v_ref, table_ref, out_ref):
    for m, (ar, ai) in enumerate(cols_out(v_ref, table_ref)):
        cut = pl.ds(256 * m, 256)
        out_ref[0, :, cut] = ar.astype(bf16)
        out_ref[1, :, cut] = ai.astype(bf16)


def call(kernel, name, outs, args, flops, scratch=()):
    size = sum(a.size * a.dtype.itemsize for a in args)
    return pl.pallas_call(
        kernel,
        name=name,
        out_shape=outs,
        in_specs=[pl.BlockSpec(memory_space=pltpu.VMEM)] * len(args),
        out_specs=jax.tree.map(lambda _: pl.BlockSpec(memory_space=pltpu.VMEM), outs),
        scratch_shapes=list(scratch),
        compiler_params=pltpu.CompilerParams(vmem_limit_bytes=VMEM_LIMIT),
        cost_estimate=pl.CostEstimate(flops=flops, bytes_accessed=size, transcendentals=0),
    )(*args)


def shape(dims, dtype):
    return jax.ShapeDtypeStruct(dims, dtype)


FLOPS = 4 * 2 * 512 * 256 * 256


def local(field_in, target, phase, moment, second):
    tab = {name: jnp.asarray(value) for name, value in host_tables().items()}
    h = transfer(lax.axis_index("row"))
    rows_tab = (tab["row_in"], tab["row_out"], tab["lane_in"], tab["lane_out"], tab["twist"], h)
    field = field_in.reshape(2, 128, N)
    goal = target.reshape(2, 128, N)

    def swap(x):
        return lax.all_to_all(x, "row", split_axis=0, concat_axis=0, tiled=True)

    chunk = shape((64, 32, 128), bf16)
    plane = shape((2, 128, N), bf16)
    t_one = swap(call(target_in_kernel, "target_in", chunk, (goal, tab["col_left"]), FLOPS))
    whole_phase = lax.all_gather(phase, "beam", axis=1, tiled=True)
    f_one = swap(
        call(field_in_kernel, "field_in", chunk, (field, whole_phase, tab["col_left"]), FLOPS)
    )
    t_two = swap(call(target_rows_kernel, "target_rows", chunk, (t_one,) + rows_tab, 3 * FLOPS))
    f_two = swap(
        call(
            field_rows_kernel,
            "field_rows",
            shape((64, 40, 128), bf16),
            (f_one, t_one) + rows_tab,
            3 * FLOPS,
        )
    )
    back, z = call(
        target_out_kernel,
        "target_out",
        (plane, shape((2, 128, N), f32)),
        (t_two, field, whole_phase, tab["col_right"]),
        FLOPS,
    )
    piece = shape((16, 256), f32)
    over, own, one, two, three = call(
        grad_kernel,
        "grad",
        (shape((2, 8), f32), piece, piece, piece, piece),
        (f_two, z),
        FLOPS // 8,
        (pltpu.VMEM((4, 16, 256), f32),),
    )
    grad = own
    for step, part in ((1, one), (2, two), (3, three)):
        grad = grad + lax.ppermute(part, "beam", [(i, i ^ step) for i in range(4)])
    forward = call(field_out_kernel, "field_out", plane, (f_two, tab["col_right"]), FLOPS)
    new_moment = 0.9 * moment + 0.1 * grad
    new_second = 0.999 * second + 0.001 * grad * grad
    corr_one = 1.0 - 0.9**STEP
    corr_two = 1.0 - 0.999**STEP
    new_phase = phase - learn_rate * (new_moment / corr_one) / (
        jnp.sqrt(new_second / corr_two) + 1e-08
    )
    split = (2, 16, 8, N)
    return (forward.reshape(split), back.reshape(split), over, new_phase, new_moment, new_second)


def solution(mesh):
    return jax.shard_map(
        local,
        mesh=mesh,
        in_specs=(
            P(None, "row", "beam", None),
            P(None, "row", "beam", None),
            P("row", "beam"),
            P("row", "beam"),
            P("row", "beam"),
        ),
        out_specs=(
            P(None, "row", "beam", None),
            P(None, "row", "beam", None),
            P(None, "beam"),
            P("row", "beam"),
            P("row", "beam"),
            P("row", "beam"),
        ),
        check_vma=False,
    )
```

```python
import functools
import math

import jax
import jax.numpy as jnp
import ml_dtypes
import numpy as np
from jax import lax
from jax.experimental import pallas as pl
from jax.experimental.pallas import tpu as pltpu
from jax.sharding import PartitionSpec as P


STEP = 10
N = 1024
BEAMS = 32
learn_rate = 0.4
f32 = jnp.float32
bf16 = jnp.bfloat16
VMEM_LIMIT = 48 * 1024 * 1024


def angles(product, size):
    turn = (product % size) * (2.0 * math.pi / size)
    return np.cos(turn), np.sin(turn)


def as_bf16(array):
    return array.astype(np.float32).astype(ml_dtypes.bfloat16)


@functools.lru_cache(None)
def host_tables():
    k = np.arange(256)
    c, s = angles(k[:, None] * k[None, :], 256)
    col_left = np.concatenate([c, s], 0) / 32.0
    col_right = np.concatenate([c, s], 1) / 32.0
    col_twist = np.stack(angles(np.arange(4)[:, None] * k[None, :], 1024), 1).astype(np.float32)
    q = np.arange(16)
    eye = np.eye(16)
    c, s = angles(q[:, None] * q[None, :], 16)
    row_left = np.concatenate([np.kron(c, eye), np.kron(s, eye)], 0) / 8.0
    kc, ks = np.kron(c, np.eye(8)) / 4.0, np.kron(s, np.eye(8)) / 4.0
    lane_in = np.block([[kc, -ks], [ks, kc]])
    lane_out = np.block([[kc, ks], [-ks, kc]])
    k1 = 4 * q[None, :, None] + np.arange(4)[:, None, None]
    r = np.repeat(q, 8)[None, None, :]
    twist = np.stack(angles(k1 * r, 1024)).astype(np.float32)
    return dict(
        col_left=as_bf16(col_left),
        col_right=as_bf16(col_right),
        col_twist=col_twist,
        row_left=as_bf16(row_left),
        lanes=as_bf16(np.stack([lane_in, lane_out])),
        twist=twist,
    )


def frequency(index):
    return jnp.where(index < N // 2, index, index - N).astype(f32)


def transfer(row_index):
    rho, a = row_index // 16, row_index % 16
    shape = (4, 16, 16, 128)
    sigma = lax.broadcasted_iota(jnp.int32, shape, 0)
    q = lax.broadcasted_iota(jnp.int32, shape, 1)
    t = lax.broadcasted_iota(jnp.int32, shape, 2)
    k2 = lax.broadcasted_iota(jnp.int32, shape, 3) // 8
    fy = frequency(4 * q + sigma + 64 * k2)
    fx = frequency(4 * (16 * a + t) + rho)
    half = float(N // 2)
    rad = (fy**2 + fx**2) / (half * half)
    theta = -60.0 * rad / (1.0 + jnp.sqrt(1.0 - 0.4 * rad))
    return jnp.stack([jnp.cos(theta), jnp.sin(theta)]).reshape(2, 4, 256, 128)


def split_four(x):
    e0 = [x[0][p] + x[2][p] for p in (0, 1)]
    e1 = [x[0][p] - x[2][p] for p in (0, 1)]
    o0 = [x[1][p] + x[3][p] for p in (0, 1)]
    o1 = [x[1][p] - x[3][p] for p in (0, 1)]
    return (
        (e0[0] + o0[0], e0[1] + o0[1]),
        (e1[0] + o1[1], e1[1] - o1[0]),
        (e0[0] - o0[0], e0[1] - o0[1]),
        (e1[0] - o1[1], e1[1] + o1[0]),
    )


def join_four(x):
    e0 = [x[0][p] + x[2][p] for p in (0, 1)]
    e1 = [x[0][p] - x[2][p] for p in (0, 1)]
    o0 = [x[1][p] + x[3][p] for p in (0, 1)]
    o1 = [x[1][p] - x[3][p] for p in (0, 1)]
    return (
        (e0[0] + o0[0], e0[1] + o0[1]),
        (e1[0] - o1[1], e1[1] + o1[0]),
        (e0[0] - o0[0], e0[1] - o0[1]),
        (e1[0] + o1[1], e1[1] - o1[0]),
    )


def dot(a, b, dims=((1,), (0,))):
    return lax.dot_general(a, b, (dims, ((), ())), preferred_element_type=f32)


def over_beams(rows):
    return jnp.broadcast_to(rows[:, None, :], (16, 8, rows.shape[1])).reshape(128, rows.shape[1])


def cols_in(parts, table_ref, twist_ref, out_ref, first):
    for rho, (ur, ui) in enumerate(split_four(parts)):
        if rho:
            c, s = twist_ref[rho, 0:1, :], twist_ref[rho, 1:2, :]
            ur, ui = ur * c + ui * s, ui * c - ur * s
        both = jnp.concatenate([ur.astype(bf16), ui.astype(bf16)], 0)
        prod = dot(table_ref[...], both, ((1,), (1,)))
        yr = prod[:256, :128] + prod[256:, 128:]
        yi = prod[:256, 128:] - prod[256:, :128]
        place = slice(16 * rho, 16 * rho + 16)
        out_ref[place, first : first + 16, :] = yr.astype(bf16).reshape(16, 16, 128)
        out_ref[place, first + 16 : first + 32, :] = yi.astype(bf16).reshape(16, 16, 128)


def target_in_kernel(x_ref, table_ref, twist_ref, out_ref):
    parts = []
    for m in range(4):
        cut = pl.ds(256 * m, 256)
        parts.append((x_ref[0, :, cut].astype(f32), x_ref[1, :, cut].astype(f32)))
    cols_in(parts, table_ref, twist_ref, out_ref, 0)


def field_in_kernel(
    x_ref, own_ref, one_ref, two_ref, three_ref, table_ref, twist_ref, goal_ref, out_ref, turn_ref
):
    me = lax.axis_index("beam")
    for step, ref in enumerate((own_ref, one_ref, two_ref, three_ref)):
        turn_ref[0, me ^ step] = jnp.cos(ref[...])
        turn_ref[1, me ^ step] = jnp.sin(ref[...])
    out_ref[:, 0:32, :] = goal_ref[...]
    parts = []
    for m in range(4):
        cut = pl.ds(256 * m, 256)
        ur, ui = x_ref[0, :, cut].astype(f32), x_ref[1, :, cut].astype(f32)
        c, s = over_beams(turn_ref[0, m]), over_beams(turn_ref[1, m])
        parts.append((ur * c - ui * s, ur * s + ui * c))
    cols_in(parts, table_ref, twist_ref, out_ref, 32)


def turn_blocks(pair, sigma, sign):
    if not sigma:
        return pair
    re, im = pair[0].reshape(16, 16, 128), pair[1].reshape(16, 16, 128)
    out_re, out_im = [], []
    for s1 in range(16):
        angle = sign * 2.0 * math.pi * sigma * s1 / 64
        c, s = math.cos(angle), math.sin(angle)
        out_re.append(re[s1] * c - im[s1] * s)
        out_im.append(re[s1] * s + im[s1] * c)
    return jnp.concatenate(out_re, 0), jnp.concatenate(out_im, 0)


def rows_pass(v_ref, first, table, lanes, twist, h_ref, sign):
    parts = []
    for m in range(4):
        cut = pl.ds(16 * m, 16)
        parts.append(
            (
                v_ref[cut, first : first + 16, :].astype(f32).reshape(256, 128),
                v_ref[cut, first + 16 : first + 32, :].astype(f32).reshape(256, 128),
            )
        )
    done = []
    for sigma, pair in enumerate(split_four(parts)):
        ur, ui = turn_blocks(pair, sigma, -1)
        prod = dot(table[...], jnp.concatenate([ur.astype(bf16), ui.astype(bf16)], 1))
        ar = (prod[:256, :128] + prod[256:, 128:]).reshape(16, 16, 128)
        ai = (prod[:256, 128:] - prod[256:, :128]).reshape(16, 16, 128)
        tc, ts = twist[0, sigma][:, None, :], twist[1, sigma][:, None, :]
        br = (ar * tc + ai * ts).astype(bf16).reshape(256, 128)
        bi = (ai * tc - ar * ts).astype(bf16).reshape(256, 128)
        spec = dot(jnp.concatenate([br, bi], 1), lanes[0])
        dr, di = spec[:, :128], spec[:, 128:]
        hc, hs = h_ref[0, sigma], h_ref[1, sigma]
        if sign > 0:
            er, ei = dr * hc - di * hs, dr * hs + di * hc
        else:
            er, ei = dr * hc + di * hs, di * hc - dr * hs
        both = jnp.concatenate([er.astype(bf16), ei.astype(bf16)], 1)
        back = dot(both, lanes[1])
        gr, gi = back[:, :128].reshape(16, 16, 128), back[:, 128:].reshape(16, 16, 128)
        hr = (gr * tc - gi * ts).astype(bf16).reshape(256, 128)
        hi = (gi * tc + gr * ts).astype(bf16).reshape(256, 128)
        prod = dot(table[...], jnp.concatenate([hr, hi], 1))
        pair = (prod[:256, :128] - prod[256:, 128:], prod[:256, 128:] + prod[256:, :128])
        done.append(turn_blocks(pair, sigma, 1))
    return join_four(done)


def rows_kernel(v_ref, table, lanes, twist, h_ref, out_ref):
    for first, sign in ((0, -1), (32, 1)):
        done = rows_pass(v_ref, first, table, lanes, twist, h_ref, sign)
        for m in range(4):
            for p in (0, 1):
                out_ref[16 * m : 16 * m + 16, first + 16 * p : first + 16 * p + 16, :] = (
                    done[m][p].astype(bf16).reshape(16, 16, 128)
                )
    sum_re = jnp.zeros((8, 128), f32)
    sum_im = jnp.zeros((8, 128), f32)
    for m in range(4):
        cut = pl.ds(16 * m, 16)
        fr, fi = done[m]
        tr = v_ref[cut, 0:16, :].astype(f32).reshape(256, 128)
        ti = v_ref[cut, 16:32, :].astype(f32).reshape(256, 128)
        sum_re = sum_re + jnp.sum((tr * fr + ti * fi).reshape(32, 8, 128), 0)
        sum_im = sum_im + jnp.sum((tr * fi - ti * fr).reshape(32, 8, 128), 0)
    re = jnp.sum(sum_re, 0, keepdims=True)
    im = jnp.sum(sum_im, 0, keepdims=True)
    re_hi, im_hi = re.astype(bf16).astype(f32), im.astype(bf16).astype(f32)
    tail = jnp.concatenate([re_hi, im_hi, re - re_hi, im - im_hi, jnp.zeros((4, 128), f32)], 0)
    out_ref[:, 64:72, :] = jnp.broadcast_to(tail.astype(bf16)[None], (64, 8, 128))


def cols_out(v_ref, first, table_ref, twist_ref):
    done = []
    for rho in range(4):
        cut = pl.ds(16 * rho, 16)
        both = jnp.concatenate(
            [
                v_ref[cut, first : first + 16, :].reshape(256, 128),
                v_ref[cut, first + 16 : first + 32, :].reshape(256, 128),
            ],
            1,
        )
        prod = dot(both, table_ref[...], ((0,), (0,)))
        qr = prod[:128, :256] - prod[128:, 256:]
        qi = prod[128:, :256] + prod[:128, 256:]
        if rho:
            c, s = twist_ref[rho, 0:1, :], twist_ref[rho, 1:2, :]
            qr, qi = qr * c - qi * s, qi * c + qr * s
        done.append((qr, qi))
    return join_four(done)


def beam_sums(v_ref):
    rows = jnp.sum(v_ref[:, 64:72, :].astype(f32), 0)
    lane = lax.broadcasted_iota(jnp.int32, (8, 128), 1) % 8
    beam = lax.broadcasted_iota(jnp.int32, (8, 128), 0)
    sums = []
    for p in (0, 1):
        line = (rows[p : p + 1] + rows[p + 2 : p + 3]) / N
        picked = jnp.where(lane == beam, jnp.broadcast_to(line, (8, 128)), 0.0)
        sums.append(jnp.sum(picked, 1, keepdims=True))
    return sums


def target_out_kernel(
    v_ref,
    x_ref,
    turn_ref,
    table_ref,
    twist_ref,
    back_ref,
    over_ref,
    own_ref,
    one_ref,
    two_ref,
    three_ref,
    whole,
):
    sums = beam_sums(v_ref)
    lanes = lax.broadcasted_iota(jnp.int32, (8, 8), 1)
    beams = lax.broadcasted_iota(jnp.int32, (8, 8), 0)
    for p in (0, 1):
        over_ref[p : p + 1, :] = jnp.sum(jnp.where(lanes == beams, sums[p], 0.0), 0, keepdims=True)
    for m, (ar, ai) in enumerate(cols_out(v_ref, 0, table_ref, twist_ref)):
        cut = pl.ds(256 * m, 256)
        c, s = over_beams(turn_ref[0, m]), over_beams(turn_ref[1, m])
        br, bi = ar * c + ai * s, ai * c - ar * s
        back_ref[0, :, cut] = br.astype(bf16)
        back_ref[1, :, cut] = bi.astype(bf16)
        ur, ui = x_ref[0, :, cut].astype(f32), x_ref[1, :, cut].astype(f32)
        zr = (br * ur + bi * ui).reshape(16, 8, 256)
        zi = (br * ui - bi * ur).reshape(16, 8, 256)
        whole[m] = -(2.0 / BEAMS) * jnp.sum(sums[0][None] * zi - sums[1][None] * zr, 1)
    me = lax.axis_index("beam")
    for step, ref in enumerate((own_ref, one_ref, two_ref, three_ref)):
        ref[...] = whole[me ^ step]


def field_out_kernel(v_ref, table_ref, twist_ref, out_ref):
    for m, (ar, ai) in enumerate(cols_out(v_ref, 32, table_ref, twist_ref)):
        cut = pl.ds(256 * m, 256)
        out_ref[0, :, cut] = ar.astype(bf16)
        out_ref[1, :, cut] = ai.astype(bf16)


def call(kernel, name, outs, args, flops, scratch=()):
    size = sum(a.size * a.dtype.itemsize for a in args)
    return pl.pallas_call(
        kernel,
        name=name,
        out_shape=outs,
        in_specs=[pl.BlockSpec(memory_space=pltpu.VMEM)] * len(args),
        out_specs=jax.tree.map(lambda _: pl.BlockSpec(memory_space=pltpu.VMEM), outs),
        scratch_shapes=list(scratch),
        compiler_params=pltpu.CompilerParams(vmem_limit_bytes=VMEM_LIMIT),
        cost_estimate=pl.CostEstimate(flops=flops, bytes_accessed=size, transcendentals=0),
    )(*args)


def shape(dims, dtype):
    return jax.ShapeDtypeStruct(dims, dtype)


FLOPS = 4 * 2 * 512 * 256 * 256


def local(field_in, target, phase, moment, second):
    tab = {name: jnp.asarray(value) for name, value in host_tables().items()}
    field = field_in.reshape(2, 128, N)
    goal = target.reshape(2, 128, N)

    def swap(x):
        return lax.all_to_all(x, "row", split_axis=0, concat_axis=0, tiled=True)

    def trade(x, step):
        return lax.ppermute(x, "beam", [(i, i ^ step) for i in range(4)])

    plane = shape((2, 128, N), bf16)
    piece = shape((16, 256), f32)
    phases = (phase,) + tuple(trade(phase, step) for step in (1, 2, 3))
    left = (tab["col_left"], tab["col_twist"])
    right = (tab["col_right"], tab["col_twist"])
    goal_cols = call(target_in_kernel, "target_in", shape((64, 32, 128), bf16), (goal,) + left, FLOPS)
    cols, turn = call(
        field_in_kernel,
        "field_in",
        (shape((64, 64, 128), bf16), shape((2, 4, 16, 256), f32)),
        (field,) + phases + left + (goal_cols,),
        FLOPS,
    )
    cols = swap(cols)
    h = transfer(lax.axis_index("row"))
    spread = call(
        rows_kernel,
        "rows",
        shape((64, 72, 128), bf16),
        (cols, tab["row_left"], tab["lanes"], tab["twist"], h),
        6 * FLOPS,
    )
    spread = swap(spread)
    back, over, own, one, two, three = call(
        target_out_kernel,
        "target_out",
        (plane, shape((2, 8), f32), piece, piece, piece, piece),
        (spread, field, turn) + right,
        FLOPS,
        (pltpu.VMEM((4, 16, 256), f32),),
    )
    grad = own + trade(one, 1) + trade(two, 2) + trade(three, 3)
    forward = call(field_out_kernel, "field_out", plane, (spread,) + right, FLOPS)
    new_moment = 0.9 * moment + 0.1 * grad
    new_second = 0.999 * second + 0.001 * grad * grad
    corr_one = 1.0 - 0.9**STEP
    corr_two = 1.0 - 0.999**STEP
    new_phase = phase - learn_rate * (new_moment / corr_one) / (
        jnp.sqrt(new_second / corr_two) + 1e-08
    )
    split = (2, 16, 8, N)
    return (forward.reshape(split), back.reshape(split), over, new_phase, new_moment, new_second)


def solution(mesh):
    return jax.shard_map(
        local,
        mesh=mesh,
        in_specs=(
            P(None, "row", "beam", None),
            P(None, "row", "beam", None),
            P("row", "beam"),
            P("row", "beam"),
            P("row", "beam"),
        ),
        out_specs=(
            P(None, "row", "beam", None),
            P(None, "row", "beam", None),
            P(None, "beam"),
            P("row", "beam"),
            P("row", "beam"),
            P("row", "beam"),
        ),
        check_vma=False,
    )
```

```python
import functools
import math

import jax
import jax.numpy as jnp
import ml_dtypes
import numpy as np
from jax import lax
from jax.experimental import pallas as pl
from jax.experimental.pallas import tpu as pltpu
from jax.sharding import PartitionSpec as P


STEP = 10
N = 1024
BEAMS = 32
learn_rate = 0.4
f32 = jnp.float32
bf16 = jnp.bfloat16
VMEM_LIMIT = 48 * 1024 * 1024


def angles(product, size):
    turn = (product % size) * (2.0 * math.pi / size)
    return np.cos(turn), np.sin(turn)


def as_bf16(array):
    return array.astype(np.float32).astype(ml_dtypes.bfloat16)


LIFT = 1.1328125
FITTED = 1.13280406


@functools.lru_cache(None)
def host_tables():
    k = np.arange(256)
    left, right = [], []
    for rho in range(3):
        c, s = angles((4 * k[:, None] + rho) * k[None, :], 1024)
        left.append(np.concatenate([c, s], 0) / 32.0)
        right.append(np.concatenate([c, s], 1) / 32.0)
    q = np.arange(16)
    c, s = angles(q[:, None] * q[None, :], 16)
    kc, ks = np.kron(c * LIFT, np.eye(8)), np.kron(s * LIFT, np.eye(8))
    lane_in = np.block([[kc, -ks], [ks, kc]])
    lane_out = np.block([[kc, ks], [-ks, kc]])
    k1 = 4 * q[None, :, None] + np.arange(4)[:, None, None]
    r = np.repeat(q, 8)[None, None, :]
    twist = np.stack(angles(k1 * r, 1024)).astype(np.float32)
    return dict(
        col_left=as_bf16(np.stack(left)),
        col_right=as_bf16(np.stack(right)),
        lanes=as_bf16(np.stack([lane_in, lane_out])),
        twist=twist,
    )


def frequency(index):
    return jnp.where(index < N // 2, index, index - N).astype(f32)


def transfer(row_index):
    rho, a = row_index // 16, row_index % 16
    shape = (4, 16, 16, 128)
    sigma = lax.broadcasted_iota(jnp.int32, shape, 0)
    q = lax.broadcasted_iota(jnp.int32, shape, 1)
    t = lax.broadcasted_iota(jnp.int32, shape, 2)
    k2 = lax.broadcasted_iota(jnp.int32, shape, 3) // 8
    fy = frequency(4 * q + sigma + 64 * k2)
    k = 4 * (16 * a + t)
    fx = frequency(jnp.where(rho == 3, 1023 - k, k + rho))
    half = float(N // 2)
    rad = (fy**2 + fx**2) / (half * half)
    theta = -60.0 * rad / (1.0 + jnp.sqrt(1.0 - 0.4 * rad))
    scale = 1.0 / (N * FITTED * FITTED)
    return jnp.stack([jnp.cos(theta) * scale, jnp.sin(theta) * scale]).reshape(2, 4, 256, 128)


def split_four(x):
    e0 = [x[0][p] + x[2][p] for p in (0, 1)]
    e1 = [x[0][p] - x[2][p] for p in (0, 1)]
    o0 = [x[1][p] + x[3][p] for p in (0, 1)]
    o1 = [x[1][p] - x[3][p] for p in (0, 1)]
    return (
        (e0[0] + o0[0], e0[1] + o0[1]),
        (e1[0] + o1[1], e1[1] - o1[0]),
        (e0[0] - o0[0], e0[1] - o0[1]),
        (e1[0] - o1[1], e1[1] + o1[0]),
    )


def join_four(x):
    e0 = [x[0][p] + x[2][p] for p in (0, 1)]
    e1 = [x[0][p] - x[2][p] for p in (0, 1)]
    o0 = [x[1][p] + x[3][p] for p in (0, 1)]
    o1 = [x[1][p] - x[3][p] for p in (0, 1)]
    return (
        (e0[0] + o0[0], e0[1] + o0[1]),
        (e1[0] - o1[1], e1[1] + o1[0]),
        (e0[0] - o0[0], e0[1] - o0[1]),
        (e1[0] + o1[1], e1[1] - o1[0]),
    )


def dot(a, b, dims=((1,), (0,))):
    return lax.dot_general(a, b, (dims, ((), ())), preferred_element_type=f32)


def over_beams(rows):
    return jnp.broadcast_to(rows[:, None, :], (16, 8, rows.shape[1])).reshape(128, rows.shape[1])


def two_bf16(x):
    high = x.astype(bf16)
    return high, (x - high.astype(f32)).astype(bf16)


def cols_in(parts, table_ref, out_ref, first):
    for rho, (ur, ui) in enumerate(split_four(parts)):
        high, low = two_bf16(jnp.concatenate([ur, ui], 0))
        left = table_ref[rho if rho < 3 else 1]
        prod = dot(left, high, ((1,), (1,))) + dot(left, low, ((1,), (1,)))
        sign = -1 if rho == 3 else 1
        yr = prod[:256, :128] + sign * prod[256:, 128:]
        yi = prod[:256, 128:] - sign * prod[256:, :128]
        place = slice(16 * rho, 16 * rho + 16)
        out_ref[place, first : first + 16, :] = yr.astype(bf16).reshape(16, 16, 128)
        out_ref[place, first + 16 : first + 32, :] = yi.astype(bf16).reshape(16, 16, 128)


def target_in_kernel(x_ref, table_ref, out_ref):
    parts = []
    for m in range(4):
        cut = pl.ds(256 * m, 256)
        parts.append((x_ref[0, :, cut].astype(f32), x_ref[1, :, cut].astype(f32)))
    cols_in(parts, table_ref, out_ref, 0)


def field_in_kernel(
    x_ref, own_ref, one_ref, two_ref, three_ref, table_ref, half_ref, out_ref, turn_ref
):
    me = lax.axis_index("beam")
    for step, ref in enumerate((own_ref, one_ref, two_ref, three_ref)):
        turn_ref[0, me ^ step] = jnp.cos(ref[...])
        turn_ref[1, me ^ step] = jnp.sin(ref[...])
    out_ref[:, 0:32, :] = half_ref[...]
    parts = []
    for m in range(4):
        cut = pl.ds(256 * m, 256)
        ur, ui = x_ref[0, :, cut].astype(f32), x_ref[1, :, cut].astype(f32)
        c, s = over_beams(turn_ref[0, m]), over_beams(turn_ref[1, m])
        wr, wi = ur * c - ui * s, ur * s + ui * c
        parts.append((wr.astype(bf16).astype(f32), wi.astype(bf16).astype(f32)))
    cols_in(parts, table_ref, out_ref, 32)


def turned(pair, part, sign):
    if part == 0:
        return pair
    c = math.cos(2.0 * math.pi * part)
    s = sign * math.sin(2.0 * math.pi * part)
    return pair[0] * c - pair[1] * s, pair[0] * s + pair[1] * c


def sixteen(x, sign):
    four = split_four if sign < 0 else join_four
    low = [four([x[i + 4 * j] for j in range(4)]) for i in range(4)]
    out = [None] * 16
    for k in range(4):
        for j, pair in enumerate(four([turned(low[i][k], i * k / 16, sign) for i in range(4)])):
            out[k + 4 * j] = pair
    return out


def stacked(pairs):
    return [jnp.concatenate([pair[p] for pair in pairs], 0) for p in (0, 1)]


def rows_pass(v_ref, first, lanes, twist, h_ref, sign):
    quads = []
    for s1 in range(16):
        parts = []
        for m in range(4):
            s = 16 * m + s1
            parts.append(
                (
                    v_ref[s, first : first + 16, :].astype(f32),
                    v_ref[s, first + 16 : first + 32, :].astype(f32),
                )
            )
        quads.append(split_four(parts))
    done = []
    for sigma in range(4):
        got = sixteen([turned(quads[s1][sigma], sigma * s1 / 64, -1) for s1 in range(16)], -1)
        spun = []
        for q in range(16):
            tc, ts = twist[0, sigma, q : q + 1, :], twist[1, sigma, q : q + 1, :]
            ar, ai = got[q]
            spun.append(((ar * tc + ai * ts).astype(bf16), (ai * tc - ar * ts).astype(bf16)))
        spec = dot(jnp.concatenate(stacked(spun), 1), lanes[0])
        dr, di = spec[:, :128], spec[:, 128:]
        hc, hs = h_ref[0, sigma], h_ref[1, sigma]
        if sign > 0:
            er, ei = dr * hc - di * hs, dr * hs + di * hc
        else:
            er, ei = dr * hc + di * hs, di * hc - dr * hs
        back = dot(jnp.concatenate([er.astype(bf16), ei.astype(bf16)], 1), lanes[1])
        spun = []
        for q in range(16):
            tc, ts = twist[0, sigma, q : q + 1, :], twist[1, sigma, q : q + 1, :]
            gr, gi = back[16 * q : 16 * q + 16, :128], back[16 * q : 16 * q + 16, 128:]
            spun.append((gr * tc - gi * ts, gi * tc + gr * ts))
        got = sixteen(spun, 1)
        done.append([turned(got[s1], sigma * s1 / 64, 1) for s1 in range(16)])
    return [join_four([done[sigma][s1] for sigma in range(4)]) for s1 in range(16)]


def rows_kernel(v_ref, lanes, twist, h_ref, out_ref):
    for first, sign in ((0, -1), (32, 1)):
        done = rows_pass(v_ref, first, lanes, twist, h_ref, sign)
        for s1 in range(16):
            for m in range(4):
                for p in (0, 1):
                    out_ref[16 * m + s1, first + 16 * p : first + 16 * p + 16, :] = (
                        done[s1][m][p].astype(bf16)
                    )
    sum_re = jnp.zeros((16, 128), f32)
    sum_im = jnp.zeros((16, 128), f32)
    for s1 in range(16):
        for m in range(4):
            fr, fi = done[s1][m]
            tr = v_ref[16 * m + s1, 0:16, :].astype(f32)
            ti = v_ref[16 * m + s1, 16:32, :].astype(f32)
            sum_re = sum_re + (tr * fr + ti * fi)
            sum_im = sum_im + (tr * fi - ti * fr)
    re = jnp.sum(sum_re, 0, keepdims=True)
    im = jnp.sum(sum_im, 0, keepdims=True)
    re_hi, im_hi = re.astype(bf16).astype(f32), im.astype(bf16).astype(f32)
    tail = jnp.concatenate([re_hi, im_hi, re - re_hi, im - im_hi, jnp.zeros((4, 128), f32)], 0)
    out_ref[:, 64:72, :] = jnp.broadcast_to(tail.astype(bf16)[None], (64, 8, 128))


def cols_out(v_ref, first, table_ref):
    done = []
    for rho in range(4):
        cut = pl.ds(16 * rho, 16)
        both = jnp.concatenate(
            [
                v_ref[cut, first : first + 16, :].reshape(256, 128),
                v_ref[cut, first + 16 : first + 32, :].reshape(256, 128),
            ],
            1,
        )
        prod = dot(both, table_ref[rho if rho < 3 else 1], ((0,), (0,)))
        sign = -1 if rho == 3 else 1
        done.append(
            (
                prod[:128, :256] - sign * prod[128:, 256:],
                prod[128:, :256] + sign * prod[:128, 256:],
            )
        )
    return join_four(done)


def beam_sums(v_ref):
    rows = jnp.sum(v_ref[:, 64:72, :].astype(f32), 0)
    lane = lax.broadcasted_iota(jnp.int32, (8, 128), 1) % 8
    beam = lax.broadcasted_iota(jnp.int32, (8, 128), 0)
    sums = []
    for p in (0, 1):
        line = (rows[p : p + 1] + rows[p + 2 : p + 3]) / N
        picked = jnp.where(lane == beam, jnp.broadcast_to(line, (8, 128)), 0.0)
        sums.append(jnp.sum(picked, 1, keepdims=True))
    return sums


def target_out_kernel(
    v_ref,
    x_ref,
    turn_ref,
    table_ref,
    back_ref,
    over_ref,
    own_ref,
    one_ref,
    two_ref,
    three_ref,
    whole,
):
    sums = beam_sums(v_ref)
    lanes = lax.broadcasted_iota(jnp.int32, (8, 8), 1)
    beams = lax.broadcasted_iota(jnp.int32, (8, 8), 0)
    for p in (0, 1):
        over_ref[p : p + 1, :] = jnp.sum(jnp.where(lanes == beams, sums[p], 0.0), 0, keepdims=True)
    for m, (ar, ai) in enumerate(cols_out(v_ref, 0, table_ref)):
        cut = pl.ds(256 * m, 256)
        c, s = over_beams(turn_ref[0, m]), over_beams(turn_ref[1, m])
        br, bi = ar * c + ai * s, ai * c - ar * s
        back_ref[0, :, cut] = br.astype(bf16)
        back_ref[1, :, cut] = bi.astype(bf16)
        ur, ui = x_ref[0, :, cut].astype(f32), x_ref[1, :, cut].astype(f32)
        zr = (br * ur + bi * ui).reshape(16, 8, 256)
        zi = (br * ui - bi * ur).reshape(16, 8, 256)
        whole[m] = -(2.0 / BEAMS) * jnp.sum(sums[0][None] * zi - sums[1][None] * zr, 1)
    me = lax.axis_index("beam")
    for step, ref in enumerate((own_ref, one_ref, two_ref, three_ref)):
        ref[...] = whole[me ^ step]


def field_out_kernel(v_ref, table_ref, out_ref):
    for m, (ar, ai) in enumerate(cols_out(v_ref, 32, table_ref)):
        cut = pl.ds(256 * m, 256)
        out_ref[0, :, cut] = ar.astype(bf16)
        out_ref[1, :, cut] = ai.astype(bf16)


def call(kernel, name, outs, args, flops, scratch=()):
    in_vmem = pl.BlockSpec(memory_space=pltpu.VMEM)
    size = sum(a.size * a.dtype.itemsize for a in args)
    return pl.pallas_call(
        kernel,
        name=name,
        out_shape=outs,
        in_specs=[in_vmem] * len(args),
        out_specs=jax.tree.map(lambda _: in_vmem, outs),
        scratch_shapes=list(scratch),
        compiler_params=pltpu.CompilerParams(vmem_limit_bytes=VMEM_LIMIT),
        cost_estimate=pl.CostEstimate(flops=flops, bytes_accessed=size, transcendentals=0),
    )(*args)


def shape(dims, dtype):
    return jax.ShapeDtypeStruct(dims, dtype)


FLOPS = 4 * 2 * 512 * 256 * 256


def local(field_in, target, phase, moment, second):
    tab = {name: jnp.asarray(value) for name, value in host_tables().items()}
    field = field_in.reshape(2, 128, N)
    goal = target.reshape(2, 128, N)

    def swap(x):
        return lax.all_to_all(x, "row", split_axis=0, concat_axis=0, tiled=True)

    def trade(x, step):
        return lax.ppermute(x, "beam", [(i, i ^ step) for i in range(4)])

    plane = shape((2, 128, N), bf16)
    piece = shape((16, 256), f32)
    phases = (phase,) + tuple(trade(phase, step) for step in (1, 2, 3))
    half = call(
        target_in_kernel,
        "target_in",
        shape((64, 32, 128), bf16),
        (goal, tab["col_left"]),
        FLOPS,
    )
    cols, turn = call(
        field_in_kernel,
        "field_in",
        (shape((64, 64, 128), bf16), shape((2, 4, 16, 256), f32)),
        (field,) + phases + (tab["col_left"], half),
        FLOPS,
    )
    cols = swap(cols)
    h = transfer(lax.axis_index("row"))
    spread = call(
        rows_kernel,
        "rows",
        shape((64, 72, 128), bf16),
        (cols, tab["lanes"], tab["twist"], h),
        6 * FLOPS,
    )
    spread = swap(spread)
    back, over, own, one, two, three = call(
        target_out_kernel,
        "target_out",
        (plane, shape((2, 8), f32), piece, piece, piece, piece),
        (spread, field, turn, tab["col_right"]),
        FLOPS,
        (pltpu.VMEM((4, 16, 256), f32),),
    )
    grad = own + trade(one, 1) + trade(two, 2) + trade(three, 3)
    forward = call(field_out_kernel, "field_out", plane, (spread, tab["col_right"]), FLOPS)
    new_moment = 0.9 * moment + 0.1 * grad
    new_second = 0.999 * second + 0.001 * grad * grad
    corr_one = 1.0 - 0.9**STEP
    corr_two = 1.0 - 0.999**STEP
    new_phase = phase - learn_rate * (new_moment / corr_one) / (
        jnp.sqrt(new_second / corr_two) + 1e-08
    )
    split = (2, 16, 8, N)
    return (forward.reshape(split), back.reshape(split), over, new_phase, new_moment, new_second)


def solution(mesh):
    return jax.shard_map(
        local,
        mesh=mesh,
        in_specs=(
            P(None, "row", "beam", None),
            P(None, "row", "beam", None),
            P("row", "beam"),
            P("row", "beam"),
            P("row", "beam"),
        ),
        out_specs=(
            P(None, "row", "beam", None),
            P(None, "row", "beam", None),
            P(None, "beam"),
            P("row", "beam"),
            P("row", "beam"),
            P("row", "beam"),
        ),
        check_vma=False,
    )
```

```python
import functools
import math

import jax
import jax.numpy as jnp
import ml_dtypes
import numpy as np
from jax import lax
from jax.experimental import pallas as pl
from jax.experimental.pallas import tpu as pltpu
from jax.sharding import PartitionSpec as P


STEP = 10
N = 1024
BEAMS = 32
learn_rate = 0.4
f32 = jnp.float32
bf16 = jnp.bfloat16
VMEM_LIMIT = 48 * 1024 * 1024


def angles(product, size):
    turn = (product % size) * (2.0 * math.pi / size)
    return np.cos(turn), np.sin(turn)


def as_bf16(array):
    return array.astype(np.float32).astype(ml_dtypes.bfloat16)


LIFT = 1.1328125
FITTED = 1.13280406


@functools.lru_cache(None)
def host_tables():
    k = np.arange(256)
    left, right = [], []
    for rho in range(3):
        c, s = angles((4 * k[:, None] + rho) * k[None, :], 1024)
        left.append(np.concatenate([c, s], 0) / 32.0)
        right.append(np.concatenate([c, s], 1) / 32.0)
    q = np.arange(16)
    c, s = angles(q[:, None] * q[None, :], 16)
    kc, ks = np.kron(c * LIFT, np.eye(8)), np.kron(s * LIFT, np.eye(8))
    lane_in = np.block([[kc, -ks], [ks, kc]])
    lane_out = np.block([[kc, ks], [-ks, kc]])
    k1 = 4 * q[None, :, None] + np.arange(4)[:, None, None]
    r = np.repeat(q, 8)[None, None, :]
    twist = np.stack(angles(k1 * r, 1024)).astype(np.float32)
    return dict(
        col_left=as_bf16(np.stack(left)),
        col_right=as_bf16(np.stack(right)),
        lanes=as_bf16(np.stack([lane_in, lane_out])),
        twist=twist,
    )


def frequency(index):
    return jnp.where(index < N // 2, index, index - N).astype(f32)


def transfer(row_index):
    rho, a = row_index // 16, row_index % 16
    shape = (4, 16, 16, 128)
    sigma = lax.broadcasted_iota(jnp.int32, shape, 0)
    q = lax.broadcasted_iota(jnp.int32, shape, 1)
    t = lax.broadcasted_iota(jnp.int32, shape, 2)
    k2 = lax.broadcasted_iota(jnp.int32, shape, 3) // 8
    fy = frequency(4 * q + sigma + 64 * k2)
    k = 4 * (16 * a + t)
    fx = frequency(jnp.where(rho == 3, 1023 - k, k + rho))
    half = float(N // 2)
    rad = (fy**2 + fx**2) / (half * half)
    theta = -60.0 * rad / (1.0 + jnp.sqrt(1.0 - 0.4 * rad))
    scale = 1.0 / (N * FITTED * FITTED)
    return jnp.stack([jnp.cos(theta) * scale, jnp.sin(theta) * scale]).reshape(2, 4, 256, 128)


def split_four(x):
    e0 = [x[0][p] + x[2][p] for p in (0, 1)]
    e1 = [x[0][p] - x[2][p] for p in (0, 1)]
    o0 = [x[1][p] + x[3][p] for p in (0, 1)]
    o1 = [x[1][p] - x[3][p] for p in (0, 1)]
    return (
        (e0[0] + o0[0], e0[1] + o0[1]),
        (e1[0] + o1[1], e1[1] - o1[0]),
        (e0[0] - o0[0], e0[1] - o0[1]),
        (e1[0] - o1[1], e1[1] + o1[0]),
    )


def join_four(x):
    e0 = [x[0][p] + x[2][p] for p in (0, 1)]
    e1 = [x[0][p] - x[2][p] for p in (0, 1)]
    o0 = [x[1][p] + x[3][p] for p in (0, 1)]
    o1 = [x[1][p] - x[3][p] for p in (0, 1)]
    return (
        (e0[0] + o0[0], e0[1] + o0[1]),
        (e1[0] - o1[1], e1[1] + o1[0]),
        (e0[0] - o0[0], e0[1] - o0[1]),
        (e1[0] + o1[1], e1[1] - o1[0]),
    )


def dot(a, b, dims=((1,), (0,))):
    return lax.dot_general(a, b, (dims, ((), ())), preferred_element_type=f32)


def over_beams(rows):
    return jnp.broadcast_to(rows[:, None, :], (16, 8, rows.shape[1])).reshape(128, rows.shape[1])


def two_bf16(x):
    high = x.astype(bf16)
    return high, (x - high.astype(f32)).astype(bf16)


def cols_in(parts, table_ref, out_ref, ready=lambda rho: None):
    for rho, (ur, ui) in enumerate(split_four(parts)):
        high, low = two_bf16(jnp.concatenate([ur, ui], 0))
        left = table_ref[rho if rho < 3 else 1]
        prod = dot(left, high, ((1,), (1,))) + dot(left, low, ((1,), (1,)))
        sign = -1 if rho == 3 else 1
        yr = prod[:256, :128] + sign * prod[256:, 128:]
        yi = prod[:256, 128:] - sign * prod[256:, :128]
        place = slice(16 * rho, 16 * rho + 16)
        out_ref[place, 0:16, :] = yr.astype(bf16).reshape(16, 16, 128)
        out_ref[place, 16:32, :] = yi.astype(bf16).reshape(16, 16, 128)
        ready(rho)


def target_in_kernel(x_ref, table_ref, out_ref):
    parts = []
    for m in range(4):
        cut = pl.ds(256 * m, 256)
        parts.append((x_ref[0, :, cut].astype(f32), x_ref[1, :, cut].astype(f32)))
    cols_in(parts, table_ref, out_ref)


def field_in_kernel(
    x_ref,
    own_ref,
    one_ref,
    two_ref,
    three_ref,
    table_ref,
    half_ref,
    far_ref,
    turn_ref,
    out_ref,
    sems,
):
    copies = [pltpu.make_async_copy(half_ref, far_ref.at[:, 0:32, :], sems.at[4])]
    copies[0].start()
    me = lax.axis_index("beam")
    for step, ref in enumerate((own_ref, one_ref, two_ref, three_ref)):
        turn_ref[0, me ^ step] = jnp.cos(ref[...])
        turn_ref[1, me ^ step] = jnp.sin(ref[...])
    parts = []
    for m in range(4):
        cut = pl.ds(256 * m, 256)
        ur, ui = x_ref[0, :, cut].astype(f32), x_ref[1, :, cut].astype(f32)
        c, s = over_beams(turn_ref[0, m]), over_beams(turn_ref[1, m])
        wr, wi = ur * c - ui * s, ur * s + ui * c
        parts.append((wr.astype(bf16).astype(f32), wi.astype(bf16).astype(f32)))

    def ready(rho):
        place = pl.ds(16 * rho, 16)
        copy = pltpu.make_async_copy(
            out_ref.at[place], far_ref.at[place, 32:64, :], sems.at[rho]
        )
        copy.start()
        copies.append(copy)

    cols_in(parts, table_ref, out_ref, ready)
    for copy in copies:
        copy.wait()


def turned(pair, part, sign):
    if part == 0:
        return pair
    c = math.cos(2.0 * math.pi * part)
    s = sign * math.sin(2.0 * math.pi * part)
    return pair[0] * c - pair[1] * s, pair[0] * s + pair[1] * c


def sixteen(x, sign):
    four = split_four if sign < 0 else join_four
    low = [four([x[i + 4 * j] for j in range(4)]) for i in range(4)]
    out = [None] * 16
    for k in range(4):
        for j, pair in enumerate(four([turned(low[i][k], i * k / 16, sign) for i in range(4)])):
            out[k + 4 * j] = pair
    return out


def stacked(pairs):
    return [jnp.concatenate([pair[p] for pair in pairs], 0) for p in (0, 1)]


def rows_pass(v_ref, first, lanes, twist, h_ref, sign):
    quads = []
    for s1 in range(16):
        parts = []
        for m in range(4):
            s = 16 * m + s1
            parts.append(
                (
                    v_ref[s, first : first + 16, :].astype(f32),
                    v_ref[s, first + 16 : first + 32, :].astype(f32),
                )
            )
        quads.append(split_four(parts))
    done = []
    for sigma in range(4):
        got = sixteen([turned(quads[s1][sigma], sigma * s1 / 64, -1) for s1 in range(16)], -1)
        spun = []
        for q in range(16):
            tc, ts = twist[0, sigma, q : q + 1, :], twist[1, sigma, q : q + 1, :]
            ar, ai = got[q]
            spun.append(((ar * tc + ai * ts).astype(bf16), (ai * tc - ar * ts).astype(bf16)))
        spec = dot(jnp.concatenate(stacked(spun), 1), lanes[0])
        dr, di = spec[:, :128], spec[:, 128:]
        hc, hs = h_ref[0, sigma], h_ref[1, sigma]
        if sign > 0:
            er, ei = dr * hc - di * hs, dr * hs + di * hc
        else:
            er, ei = dr * hc + di * hs, di * hc - dr * hs
        back = dot(jnp.concatenate([er.astype(bf16), ei.astype(bf16)], 1), lanes[1])
        spun = []
        for q in range(16):
            tc, ts = twist[0, sigma, q : q + 1, :], twist[1, sigma, q : q + 1, :]
            gr, gi = back[16 * q : 16 * q + 16, :128], back[16 * q : 16 * q + 16, 128:]
            spun.append((gr * tc - gi * ts, gi * tc + gr * ts))
        got = sixteen(spun, 1)
        done.append([turned(got[s1], sigma * s1 / 64, 1) for s1 in range(16)])
    return [join_four([done[sigma][s1] for sigma in range(4)]) for s1 in range(16)]


def rows_kernel(v_ref, lanes, twist, h_ref, far_ref, pairs, sems):
    out_ref = pairs.reshape(64, 66, 128)
    copies = []
    for first, sign in ((0, -1), (32, 1)):
        done = rows_pass(v_ref, first, lanes, twist, h_ref, sign)
        for s1 in range(16):
            for m in range(4):
                for p in (0, 1):
                    out_ref[16 * m + s1, first + 16 * p : first + 16 * p + 16, :] = (
                        done[s1][m][p].astype(bf16)
                    )
        if not first:
            copies.append(
                pltpu.make_async_copy(pairs.at[:, 0:16], far_ref.at[:, 0:16], sems.at[0])
            )
            copies[0].start()
    sum_re = jnp.zeros((16, 128), f32)
    sum_im = jnp.zeros((16, 128), f32)
    for s1 in range(16):
        for m in range(4):
            fr, fi = done[s1][m]
            tr = v_ref[16 * m + s1, 0:16, :].astype(f32)
            ti = v_ref[16 * m + s1, 16:32, :].astype(f32)
            sum_re = sum_re + (tr * fr + ti * fi)
            sum_im = sum_im + (tr * fi - ti * fr)
    re = jnp.sum(sum_re, 0, keepdims=True)
    im = jnp.sum(sum_im, 0, keepdims=True)
    both = jnp.concatenate([re, im], 0)
    both = both + pltpu.roll(both, 64, 1)
    high = both.astype(bf16).astype(f32)
    lane = lax.broadcasted_iota(jnp.int32, (2, 128), 1)
    tail = jnp.where(lane < 64, high, both - high).astype(bf16)
    out_ref[:, 64:66, :] = jnp.broadcast_to(tail[None], (64, 2, 128))
    copies.append(pltpu.make_async_copy(pairs.at[:, 16:33], far_ref.at[:, 16:33], sems.at[1]))
    copies[1].start()
    for copy in copies:
        copy.wait()


def cols_out(pairs_ref, first, table_ref):
    v_ref = pairs_ref.reshape(64, 66, 128)
    done = []
    for rho in range(4):
        cut = pl.ds(16 * rho, 16)
        both = jnp.concatenate(
            [
                v_ref[cut, first : first + 16, :].reshape(256, 128),
                v_ref[cut, first + 16 : first + 32, :].reshape(256, 128),
            ],
            1,
        )
        prod = dot(both, table_ref[rho if rho < 3 else 1], ((0,), (0,)))
        sign = -1 if rho == 3 else 1
        done.append(
            (
                prod[:128, :256] - sign * prod[128:, 256:],
                prod[128:, :256] + sign * prod[:128, 256:],
            )
        )
    return join_four(done)


def beam_sums(pairs_ref):
    rows = jnp.sum(pairs_ref[:, 32, :, :].astype(f32), 0)
    lane = lax.broadcasted_iota(jnp.int32, (8, 128), 1) % 8
    beam = lax.broadcasted_iota(jnp.int32, (8, 128), 0)
    sums = []
    for p in (0, 1):
        line = rows[p : p + 1] / N
        picked = jnp.where(lane == beam, jnp.broadcast_to(line, (8, 128)), 0.0)
        sums.append(jnp.sum(picked, 1, keepdims=True))
    return sums


def target_out_kernel(
    v_ref,
    x_ref,
    turn_ref,
    table_ref,
    back_ref,
    over_ref,
    own_ref,
    one_ref,
    two_ref,
    three_ref,
    whole,
):
    sums = beam_sums(v_ref)
    lanes = lax.broadcasted_iota(jnp.int32, (8, 8), 1)
    beams = lax.broadcasted_iota(jnp.int32, (8, 8), 0)
    for p in (0, 1):
        over_ref[p : p + 1, :] = jnp.sum(jnp.where(lanes == beams, sums[p], 0.0), 0, keepdims=True)
    for m, (ar, ai) in enumerate(cols_out(v_ref, 0, table_ref)):
        cut = pl.ds(256 * m, 256)
        c, s = over_beams(turn_ref[0, m]), over_beams(turn_ref[1, m])
        br, bi = ar * c + ai * s, ai * c - ar * s
        back_ref[0, :, cut] = br.astype(bf16)
        back_ref[1, :, cut] = bi.astype(bf16)
        ur, ui = x_ref[0, :, cut].astype(f32), x_ref[1, :, cut].astype(f32)
        zr = (br * ur + bi * ui).reshape(16, 8, 256)
        zi = (br * ui - bi * ur).reshape(16, 8, 256)
        whole[m] = -(2.0 / BEAMS) * jnp.sum(sums[0][None] * zi - sums[1][None] * zr, 1)
    me = lax.axis_index("beam")
    for step, ref in enumerate((own_ref, one_ref, two_ref, three_ref)):
        ref[...] = whole[me ^ step]


def field_out_kernel(v_ref, table_ref, out_ref):
    for m, (ar, ai) in enumerate(cols_out(v_ref, 32, table_ref)):
        cut = pl.ds(256 * m, 256)
        out_ref[0, :, cut] = ar.astype(bf16)
        out_ref[1, :, cut] = ai.astype(bf16)


def call(kernel, name, outs, args, flops, scratch=(), far=()):
    in_vmem = pl.BlockSpec(memory_space=pltpu.VMEM)
    in_hbm = pl.BlockSpec(memory_space=pltpu.HBM)
    many = isinstance(outs, tuple)
    specs = tuple(in_hbm if i in far else in_vmem for i in range(len(outs) if many else 1))
    size = sum(a.size * a.dtype.itemsize for a in args)
    return pl.pallas_call(
        kernel,
        name=name,
        out_shape=outs,
        in_specs=[in_vmem] * len(args),
        out_specs=specs if many else specs[0],
        scratch_shapes=list(scratch),
        compiler_params=pltpu.CompilerParams(vmem_limit_bytes=VMEM_LIMIT),
        cost_estimate=pl.CostEstimate(flops=flops, bytes_accessed=size, transcendentals=0),
    )(*args)


def shape(dims, dtype):
    return jax.ShapeDtypeStruct(dims, dtype)


FLOPS = 4 * 2 * 512 * 256 * 256


def local(field_in, target, phase, moment, second):
    tab = {name: jnp.asarray(value) for name, value in host_tables().items()}
    field = field_in.reshape(2, 128, N)
    goal = target.reshape(2, 128, N)

    def swap(x):
        return lax.all_to_all(x, "row", split_axis=0, concat_axis=0, tiled=True)

    def trade(x, step):
        return lax.ppermute(x, "beam", [(i, i ^ step) for i in range(4)])

    plane = shape((2, 128, N), bf16)
    piece = shape((16, 256), f32)
    phases = (phase,) + tuple(trade(phase, step) for step in (1, 2, 3))
    half = call(
        target_in_kernel,
        "target_in",
        shape((64, 32, 128), bf16),
        (goal, tab["col_left"]),
        FLOPS,
    )
    cols, turn = call(
        field_in_kernel,
        "field_in",
        (shape((64, 64, 128), bf16), shape((2, 4, 16, 256), f32)),
        (field,) + phases + (tab["col_left"], half),
        FLOPS,
        (pltpu.VMEM((64, 32, 128), bf16), pltpu.SemaphoreType.DMA((5,))),
        (0,),
    )
    cols = swap(cols)
    h = transfer(lax.axis_index("row"))
    spread = call(
        rows_kernel,
        "rows",
        shape((64, 33, 2, 128), bf16),
        (cols, tab["lanes"], tab["twist"], h),
        6 * FLOPS,
        (pltpu.VMEM((64, 33, 2, 128), bf16), pltpu.SemaphoreType.DMA((2,))),
        (0,),
    )
    spread = swap(spread)
    back, over, own, one, two, three = call(
        target_out_kernel,
        "target_out",
        (plane, shape((2, 8), f32), piece, piece, piece, piece),
        (spread, field, turn, tab["col_right"]),
        FLOPS,
        (pltpu.VMEM((4, 16, 256), f32),),
    )
    grad = own + trade(one, 1) + trade(two, 2) + trade(three, 3)
    forward = call(field_out_kernel, "field_out", plane, (spread, tab["col_right"]), FLOPS)
    new_moment = 0.9 * moment + 0.1 * grad
    new_second = 0.999 * second + 0.001 * grad * grad
    corr_one = 1.0 - 0.9**STEP
    corr_two = 1.0 - 0.999**STEP
    new_phase = phase - learn_rate * (new_moment / corr_one) / (
        jnp.sqrt(new_second / corr_two) + 1e-08
    )
    split = (2, 16, 8, N)
    return (forward.reshape(split), back.reshape(split), over, new_phase, new_moment, new_second)


def solution(mesh):
    return jax.shard_map(
        local,
        mesh=mesh,
        in_specs=(
            P(None, "row", "beam", None),
            P(None, "row", "beam", None),
            P("row", "beam"),
            P("row", "beam"),
            P("row", "beam"),
        ),
        out_specs=(
            P(None, "row", "beam", None),
            P(None, "row", "beam", None),
            P(None, "beam"),
            P("row", "beam"),
            P("row", "beam"),
            P("row", "beam"),
        ),
        check_vma=False,
    )
```

```python
import functools
import math

import jax
import jax.numpy as jnp
import ml_dtypes
import numpy as np
from jax import lax
from jax.experimental import pallas as pl
from jax.experimental.pallas import tpu as pltpu
from jax.sharding import PartitionSpec as P


STEP = 10
N = 1024
BEAMS = 32
learn_rate = 0.4
f32 = jnp.float32
bf16 = jnp.bfloat16
VMEM_LIMIT = 48 * 1024 * 1024


def angles(product, size):
    turn = (product % size) * (2.0 * math.pi / size)
    return np.cos(turn), np.sin(turn)


def as_bf16(array):
    return array.astype(np.float32).astype(ml_dtypes.bfloat16)


LIFT = 1.1328125
FITTED = 1.13280406


@functools.lru_cache(None)
def host_tables():
    k = np.arange(256)
    left, right = [], []
    for rho in range(3):
        c, s = angles((4 * k[:, None] + rho) * k[None, :], 1024)
        left.append(np.concatenate([c, s], 0) / 32.0)
        right.append(np.concatenate([c, s], 1) / 32.0)
    q = np.arange(16)
    c, s = angles(q[:, None] * q[None, :], 16)
    kc, ks = np.kron(c * LIFT, np.eye(8)), np.kron(s * LIFT, np.eye(8))
    lane_in = np.block([[kc, -ks], [ks, kc]])
    lane_out = np.block([[kc, ks], [-ks, kc]])
    k1 = 4 * q[None, :, None] + np.arange(4)[:, None, None]
    r = np.repeat(q, 8)[None, None, :]
    twist = np.stack(angles(k1 * r, 1024)).astype(np.float32)
    return dict(
        col_left=as_bf16(np.stack(left)),
        col_right=as_bf16(np.stack(right)),
        lanes=as_bf16(np.stack([lane_in, lane_out])),
        twist=twist,
    )


def frequency(index):
    return jnp.where(index < N // 2, index, index - N).astype(f32)


def transfer(row_index):
    rho, a = row_index // 16, row_index % 16
    shape = (4, 16, 16, 128)
    sigma = lax.broadcasted_iota(jnp.int32, shape, 0)
    q = lax.broadcasted_iota(jnp.int32, shape, 1)
    t = lax.broadcasted_iota(jnp.int32, shape, 2)
    k2 = lax.broadcasted_iota(jnp.int32, shape, 3) // 8
    fy = frequency(4 * q + sigma + 64 * k2)
    k = 4 * (16 * a + t)
    fx = frequency(jnp.where(rho == 3, 1023 - k, k + rho))
    half = float(N // 2)
    rad = (fy**2 + fx**2) / (half * half)
    theta = -60.0 * rad / (1.0 + jnp.sqrt(1.0 - 0.4 * rad))
    scale = 1.0 / (N * FITTED * FITTED)
    return jnp.stack([jnp.cos(theta) * scale, jnp.sin(theta) * scale]).reshape(2, 4, 256, 128)


def split_four(x):
    e0 = [x[0][p] + x[2][p] for p in (0, 1)]
    e1 = [x[0][p] - x[2][p] for p in (0, 1)]
    o0 = [x[1][p] + x[3][p] for p in (0, 1)]
    o1 = [x[1][p] - x[3][p] for p in (0, 1)]
    return (
        (e0[0] + o0[0], e0[1] + o0[1]),
        (e1[0] + o1[1], e1[1] - o1[0]),
        (e0[0] - o0[0], e0[1] - o0[1]),
        (e1[0] - o1[1], e1[1] + o1[0]),
    )


def join_four(x):
    e0 = [x[0][p] + x[2][p] for p in (0, 1)]
    e1 = [x[0][p] - x[2][p] for p in (0, 1)]
    o0 = [x[1][p] + x[3][p] for p in (0, 1)]
    o1 = [x[1][p] - x[3][p] for p in (0, 1)]
    return (
        (e0[0] + o0[0], e0[1] + o0[1]),
        (e1[0] - o1[1], e1[1] + o1[0]),
        (e0[0] - o0[0], e0[1] - o0[1]),
        (e1[0] + o1[1], e1[1] - o1[0]),
    )


def dot(a, b, dims=((1,), (0,))):
    return lax.dot_general(a, b, (dims, ((), ())), preferred_element_type=f32)


def over_beams(rows):
    return jnp.broadcast_to(rows[:, None, :], (16, 8, rows.shape[1])).reshape(128, rows.shape[1])


def two_bf16(x):
    high = x.astype(bf16)
    return high, (x - high.astype(f32)).astype(bf16)


def cols_in(parts, table_ref, out_ref, ready=lambda rho: None):
    for rho, (ur, ui) in enumerate(split_four(parts)):
        high, low = two_bf16(jnp.concatenate([ur, ui], 0))
        left = table_ref[rho if rho < 3 else 1]
        prod = dot(left, high, ((1,), (1,))) + dot(left, low, ((1,), (1,)))
        sign = -1 if rho == 3 else 1
        yr = prod[:256, :128] + sign * prod[256:, 128:]
        yi = prod[:256, 128:] - sign * prod[256:, :128]
        place = slice(16 * rho, 16 * rho + 16)
        out_ref[place, 0:16, :] = yr.astype(bf16).reshape(16, 16, 128)
        out_ref[place, 16:32, :] = yi.astype(bf16).reshape(16, 16, 128)
        ready(rho)


def target_in_kernel(x_ref, table_ref, out_ref):
    parts = []
    for m in range(4):
        cut = pl.ds(256 * m, 256)
        parts.append((x_ref[0, :, cut].astype(f32), x_ref[1, :, cut].astype(f32)))
    cols_in(parts, table_ref, out_ref)


def field_in_kernel(
    x_ref,
    own_ref,
    one_ref,
    other_ref,
    table_ref,
    half_ref,
    far_ref,
    turn_ref,
    out_ref,
    sems,
):
    copies = [pltpu.make_async_copy(half_ref, far_ref.at[:, 0:32, :], sems.at[4])]
    copies[0].start()
    me = lax.axis_index("beam")
    for step, ref in enumerate((own_ref, one_ref, other_ref.at[0], other_ref.at[1])):
        turn_ref[0, me ^ step] = jnp.cos(ref[...])
        turn_ref[1, me ^ step] = jnp.sin(ref[...])
    parts = []
    for m in range(4):
        cut = pl.ds(256 * m, 256)
        ur, ui = x_ref[0, :, cut].astype(f32), x_ref[1, :, cut].astype(f32)
        c, s = over_beams(turn_ref[0, m]), over_beams(turn_ref[1, m])
        wr, wi = ur * c - ui * s, ur * s + ui * c
        parts.append((wr.astype(bf16).astype(f32), wi.astype(bf16).astype(f32)))

    def ready(rho):
        place = pl.ds(16 * rho, 16)
        copy = pltpu.make_async_copy(
            out_ref.at[place], far_ref.at[place, 32:64, :], sems.at[rho]
        )
        copy.start()
        copies.append(copy)

    cols_in(parts, table_ref, out_ref, ready)
    for copy in copies:
        copy.wait()


def turned(pair, part, sign):
    if part == 0:
        return pair
    c = math.cos(2.0 * math.pi * part)
    s = sign * math.sin(2.0 * math.pi * part)
    return pair[0] * c - pair[1] * s, pair[0] * s + pair[1] * c


def sixteen(x, sign):
    four = split_four if sign < 0 else join_four
    low = [four([x[i + 4 * j] for j in range(4)]) for i in range(4)]
    out = [None] * 16
    for k in range(4):
        for j, pair in enumerate(four([turned(low[i][k], i * k / 16, sign) for i in range(4)])):
            out[k + 4 * j] = pair
    return out


def stacked(pairs):
    return [jnp.concatenate([pair[p] for pair in pairs], 0) for p in (0, 1)]


def rows_pass(v_ref, first, lanes, twist, h_ref, sign):
    quads = []
    for s1 in range(16):
        parts = []
        for m in range(4):
            s = 16 * m + s1
            parts.append(
                (
                    v_ref[s, first : first + 16, :].astype(f32),
                    v_ref[s, first + 16 : first + 32, :].astype(f32),
                )
            )
        quads.append(split_four(parts))
    done = []
    for sigma in range(4):
        got = sixteen([turned(quads[s1][sigma], sigma * s1 / 64, -1) for s1 in range(16)], -1)
        spun = []
        for q in range(16):
            tc, ts = twist[0, sigma, q : q + 1, :], twist[1, sigma, q : q + 1, :]
            ar, ai = got[q]
            spun.append(((ar * tc + ai * ts).astype(bf16), (ai * tc - ar * ts).astype(bf16)))
        spec = dot(jnp.concatenate(stacked(spun), 1), lanes[0])
        dr, di = spec[:, :128], spec[:, 128:]
        hc, hs = h_ref[0, sigma], h_ref[1, sigma]
        if sign > 0:
            er, ei = dr * hc - di * hs, dr * hs + di * hc
        else:
            er, ei = dr * hc + di * hs, di * hc - dr * hs
        back = dot(jnp.concatenate([er.astype(bf16), ei.astype(bf16)], 1), lanes[1])
        spun = []
        for q in range(16):
            tc, ts = twist[0, sigma, q : q + 1, :], twist[1, sigma, q : q + 1, :]
            gr, gi = back[16 * q : 16 * q + 16, :128], back[16 * q : 16 * q + 16, 128:]
            spun.append((gr * tc - gi * ts, gi * tc + gr * ts))
        got = sixteen(spun, 1)
        done.append([turned(got[s1], sigma * s1 / 64, 1) for s1 in range(16)])
    return [join_four([done[sigma][s1] for sigma in range(4)]) for s1 in range(16)]


def rows_kernel(v_ref, lanes, twist, h_ref, far_ref, pairs, sems):
    out_ref = pairs.reshape(64, 66, 128)
    copies = []
    for first, sign in ((0, -1), (32, 1)):
        done = rows_pass(v_ref, first, lanes, twist, h_ref, sign)
        for s1 in range(16):
            for m in range(4):
                for p in (0, 1):
                    out_ref[16 * m + s1, first + 16 * p : first + 16 * p + 16, :] = (
                        done[s1][m][p].astype(bf16)
                    )
        if not first:
            copies.append(
                pltpu.make_async_copy(pairs.at[:, 0:16], far_ref.at[:, 0:16], sems.at[0])
            )
            copies[0].start()
    sum_re = jnp.zeros((16, 128), f32)
    sum_im = jnp.zeros((16, 128), f32)
    for s1 in range(16):
        for m in range(4):
            fr, fi = done[s1][m]
            tr = v_ref[16 * m + s1, 0:16, :].astype(f32)
            ti = v_ref[16 * m + s1, 16:32, :].astype(f32)
            sum_re = sum_re + (tr * fr + ti * fi)
            sum_im = sum_im + (tr * fi - ti * fr)
    re = jnp.sum(sum_re, 0, keepdims=True)
    im = jnp.sum(sum_im, 0, keepdims=True)
    both = jnp.concatenate([re, im], 0)
    both = both + pltpu.roll(both, 64, 1)
    high = both.astype(bf16).astype(f32)
    lane = lax.broadcasted_iota(jnp.int32, (2, 128), 1)
    tail = jnp.where(lane < 64, high, both - high).astype(bf16)
    out_ref[:, 64:66, :] = jnp.broadcast_to(tail[None], (64, 2, 128))
    copies.append(pltpu.make_async_copy(pairs.at[:, 16:33], far_ref.at[:, 16:33], sems.at[1]))
    copies[1].start()
    for copy in copies:
        copy.wait()


def cols_out(pairs_ref, first, table_ref):
    v_ref = pairs_ref.reshape(64, 66, 128)
    done = []
    for rho in range(4):
        cut = pl.ds(16 * rho, 16)
        both = jnp.concatenate(
            [
                v_ref[cut, first : first + 16, :].reshape(256, 128),
                v_ref[cut, first + 16 : first + 32, :].reshape(256, 128),
            ],
            1,
        )
        prod = dot(both, table_ref[rho if rho < 3 else 1], ((0,), (0,)))
        sign = -1 if rho == 3 else 1
        done.append(
            (
                prod[:128, :256] - sign * prod[128:, 256:],
                prod[128:, :256] + sign * prod[:128, 256:],
            )
        )
    return join_four(done)


def beam_sums(pairs_ref):
    rows = jnp.sum(pairs_ref[:, 32, :, :].astype(f32), 0)
    lane = lax.broadcasted_iota(jnp.int32, (8, 128), 1) % 8
    beam = lax.broadcasted_iota(jnp.int32, (8, 128), 0)
    sums = []
    for p in (0, 1):
        line = rows[p : p + 1] / N
        picked = jnp.where(lane == beam, jnp.broadcast_to(line, (8, 128)), 0.0)
        sums.append(jnp.sum(picked, 1, keepdims=True))
    return sums


def target_out_kernel(
    v_ref,
    x_ref,
    turn_ref,
    table_ref,
    back_ref,
    over_ref,
    keep_ref,
    near_ref,
    whole,
):
    sums = beam_sums(v_ref)
    lanes = lax.broadcasted_iota(jnp.int32, (8, 8), 1)
    beams = lax.broadcasted_iota(jnp.int32, (8, 8), 0)
    for p in (0, 1):
        over_ref[p : p + 1, :] = jnp.sum(jnp.where(lanes == beams, sums[p], 0.0), 0, keepdims=True)
    for m, (ar, ai) in enumerate(cols_out(v_ref, 0, table_ref)):
        cut = pl.ds(256 * m, 256)
        c, s = over_beams(turn_ref[0, m]), over_beams(turn_ref[1, m])
        br, bi = ar * c + ai * s, ai * c - ar * s
        back_ref[0, :, cut] = br.astype(bf16)
        back_ref[1, :, cut] = bi.astype(bf16)
        ur, ui = x_ref[0, :, cut].astype(f32), x_ref[1, :, cut].astype(f32)
        zr = (br * ur + bi * ui).reshape(16, 8, 256)
        zi = (br * ui - bi * ur).reshape(16, 8, 256)
        whole[m] = -(2.0 / BEAMS) * jnp.sum(sums[0][None] * zi - sums[1][None] * zr, 1)
    me = lax.axis_index("beam")
    for place, step in enumerate((0, 2)):
        keep_ref[place] = whole[me ^ step]
        near_ref[place] = whole[me ^ step ^ 1]


def field_out_kernel(v_ref, table_ref, out_ref):
    for m, (ar, ai) in enumerate(cols_out(v_ref, 32, table_ref)):
        cut = pl.ds(256 * m, 256)
        out_ref[0, :, cut] = ar.astype(bf16)
        out_ref[1, :, cut] = ai.astype(bf16)


def call(kernel, name, outs, args, flops, scratch=(), far=()):
    in_vmem = pl.BlockSpec(memory_space=pltpu.VMEM)
    in_hbm = pl.BlockSpec(memory_space=pltpu.HBM)
    many = isinstance(outs, tuple)
    specs = tuple(in_hbm if i in far else in_vmem for i in range(len(outs) if many else 1))
    size = sum(a.size * a.dtype.itemsize for a in args)
    return pl.pallas_call(
        kernel,
        name=name,
        out_shape=outs,
        in_specs=[in_vmem] * len(args),
        out_specs=specs if many else specs[0],
        scratch_shapes=list(scratch),
        compiler_params=pltpu.CompilerParams(vmem_limit_bytes=VMEM_LIMIT),
        cost_estimate=pl.CostEstimate(flops=flops, bytes_accessed=size, transcendentals=0),
    )(*args)


def shape(dims, dtype):
    return jax.ShapeDtypeStruct(dims, dtype)


FLOPS = 4 * 2 * 512 * 256 * 256


def local(field_in, target, phase, moment, second):
    tab = {name: jnp.asarray(value) for name, value in host_tables().items()}
    field = field_in.reshape(2, 128, N)
    goal = target.reshape(2, 128, N)

    def swap(x):
        return lax.all_to_all(x, "row", split_axis=0, concat_axis=0, tiled=True)

    def trade(x, step):
        return lax.ppermute(x, "beam", [(i, i ^ step) for i in range(4)])

    plane = shape((2, 128, N), bf16)
    pieces = shape((2, 16, 256), f32)
    one = trade(phase, 1)
    phases = (phase, one, trade(jnp.stack([phase, one]), 2))
    half = call(
        target_in_kernel,
        "target_in",
        shape((64, 32, 128), bf16),
        (goal, tab["col_left"]),
        FLOPS,
    )
    cols, turn = call(
        field_in_kernel,
        "field_in",
        (shape((64, 64, 128), bf16), shape((2, 4, 16, 256), f32)),
        (field,) + phases + (tab["col_left"], half),
        FLOPS,
        (pltpu.VMEM((64, 32, 128), bf16), pltpu.SemaphoreType.DMA((5,))),
        (0,),
    )
    cols = swap(cols)
    h = transfer(lax.axis_index("row"))
    spread = call(
        rows_kernel,
        "rows",
        shape((64, 33, 2, 128), bf16),
        (cols, tab["lanes"], tab["twist"], h),
        6 * FLOPS,
        (pltpu.VMEM((64, 33, 2, 128), bf16), pltpu.SemaphoreType.DMA((2,))),
        (0,),
    )
    spread = swap(spread)
    back, over, keep, near = call(
        target_out_kernel,
        "target_out",
        (plane, shape((2, 8), f32), pieces, pieces),
        (spread, field, turn, tab["col_right"]),
        FLOPS,
        (pltpu.VMEM((4, 16, 256), f32),),
    )
    mine = keep + trade(near, 1)
    grad = mine[0] + trade(mine[1], 2)
    forward = call(field_out_kernel, "field_out", plane, (spread, tab["col_right"]), FLOPS)
    new_moment = 0.9 * moment + 0.1 * grad
    new_second = 0.999 * second + 0.001 * grad * grad
    corr_one = 1.0 - 0.9**STEP
    corr_two = 1.0 - 0.999**STEP
    new_phase = phase - learn_rate * (new_moment / corr_one) / (
        jnp.sqrt(new_second / corr_two) + 1e-08
    )
    split = (2, 16, 8, N)
    return (forward.reshape(split), back.reshape(split), over, new_phase, new_moment, new_second)


def solution(mesh):
    return jax.shard_map(
        local,
        mesh=mesh,
        in_specs=(
            P(None, "row", "beam", None),
            P(None, "row", "beam", None),
            P("row", "beam"),
            P("row", "beam"),
            P("row", "beam"),
        ),
        out_specs=(
            P(None, "row", "beam", None),
            P(None, "row", "beam", None),
            P(None, "beam"),
            P("row", "beam"),
            P("row", "beam"),
            P("row", "beam"),
        ),
        check_vma=False,
    )
```

```python
import functools
import math

import jax
import jax.numpy as jnp
import ml_dtypes
import numpy as np
from jax import lax
from jax.experimental import pallas as pl
from jax.experimental.pallas import tpu as pltpu
from jax.sharding import PartitionSpec as P


STEP = 10
N = 1024
BEAMS = 32
learn_rate = 0.4
f32 = jnp.float32
bf16 = jnp.bfloat16
VMEM_LIMIT = 48 * 1024 * 1024


def angles(product, size):
    turn = (product % size) * (2.0 * math.pi / size)
    return np.cos(turn), np.sin(turn)


def as_bf16(array):
    return array.astype(np.float32).astype(ml_dtypes.bfloat16)


LIFT = 1.1328125
FITTED = 1.13280406


@functools.lru_cache(None)
def host_tables():
    k = np.arange(256)
    left, right = [], []
    for rho in range(3):
        c, s = angles((4 * k[:, None] + rho) * k[None, :], 1024)
        left.append(np.concatenate([c, s], 0) / 32.0)
        right.append(np.concatenate([c, s], 1) / 32.0)
    q = np.arange(16)
    c, s = angles(q[:, None] * q[None, :], 16)
    kc, ks = np.kron(c * LIFT, np.eye(8)), np.kron(s * LIFT, np.eye(8))
    lane_in = np.block([[kc, -ks], [ks, kc]])
    lane_out = np.block([[kc, ks], [-ks, kc]])
    k1 = 4 * q[None, :, None] + np.arange(4)[:, None, None]
    r = np.repeat(q, 8)[None, None, :]
    twist = np.stack(angles(k1 * r, 1024)).astype(np.float32)
    return dict(
        col_left=as_bf16(np.stack(left)),
        col_right=as_bf16(np.stack(right)),
        lanes=as_bf16(np.stack([lane_in, lane_out])),
        twist=twist,
    )


def frequency(index):
    return jnp.where(index < N // 2, index, index - N).astype(f32)


def transfer(row_index):
    rho, a = row_index // 16, row_index % 16
    shape = (4, 16, 16, 128)
    sigma = lax.broadcasted_iota(jnp.int32, shape, 0)
    q = lax.broadcasted_iota(jnp.int32, shape, 1)
    t = lax.broadcasted_iota(jnp.int32, shape, 2)
    k2 = lax.broadcasted_iota(jnp.int32, shape, 3) // 8
    fy = frequency(4 * q + sigma + 64 * k2)
    k = 4 * (16 * a + t)
    fx = frequency(jnp.where(rho == 3, 1023 - k, k + rho))
    half = float(N // 2)
    rad = (fy**2 + fx**2) / (half * half)
    theta = -60.0 * rad / (1.0 + jnp.sqrt(1.0 - 0.4 * rad))
    scale = 1.0 / (N * FITTED * FITTED)
    return jnp.stack([jnp.cos(theta) * scale, jnp.sin(theta) * scale]).reshape(2, 4, 256, 128)


def split_four(x):
    e0 = [x[0][p] + x[2][p] for p in (0, 1)]
    e1 = [x[0][p] - x[2][p] for p in (0, 1)]
    o0 = [x[1][p] + x[3][p] for p in (0, 1)]
    o1 = [x[1][p] - x[3][p] for p in (0, 1)]
    return (
        (e0[0] + o0[0], e0[1] + o0[1]),
        (e1[0] + o1[1], e1[1] - o1[0]),
        (e0[0] - o0[0], e0[1] - o0[1]),
        (e1[0] - o1[1], e1[1] + o1[0]),
    )


def join_four(x):
    e0 = [x[0][p] + x[2][p] for p in (0, 1)]
    e1 = [x[0][p] - x[2][p] for p in (0, 1)]
    o0 = [x[1][p] + x[3][p] for p in (0, 1)]
    o1 = [x[1][p] - x[3][p] for p in (0, 1)]
    return (
        (e0[0] + o0[0], e0[1] + o0[1]),
        (e1[0] - o1[1], e1[1] + o1[0]),
        (e0[0] - o0[0], e0[1] - o0[1]),
        (e1[0] + o1[1], e1[1] - o1[0]),
    )


def dot(a, b, dims=((1,), (0,))):
    return lax.dot_general(a, b, (dims, ((), ())), preferred_element_type=f32)


def over_beams(rows):
    return jnp.broadcast_to(rows[:, None, :], (16, 8, rows.shape[1])).reshape(128, rows.shape[1])


def two_bf16(x):
    high = x.astype(bf16)
    return high, (x - high.astype(f32)).astype(bf16)


def cols_in(parts, table_ref, out_ref, ready=lambda rho: None):
    for rho, (ur, ui) in enumerate(split_four(parts)):
        high, low = two_bf16(jnp.concatenate([ur, ui], 0))
        left = table_ref[rho if rho < 3 else 1]
        prod = dot(left, high, ((1,), (1,))) + dot(left, low, ((1,), (1,)))
        sign = -1 if rho == 3 else 1
        yr = prod[:256, :128] + sign * prod[256:, 128:]
        yi = prod[:256, 128:] - sign * prod[256:, :128]
        place = slice(16 * rho, 16 * rho + 16)
        out_ref[place, 0:16, :] = yr.astype(bf16).reshape(16, 16, 128)
        out_ref[place, 16:32, :] = yi.astype(bf16).reshape(16, 16, 128)
        ready(rho)


def target_in_kernel(x_ref, table_ref, out_ref):
    parts = []
    for m in range(4):
        cut = pl.ds(256 * m, 256)
        parts.append((x_ref[0, :, cut].astype(f32), x_ref[1, :, cut].astype(f32)))
    cols_in(parts, table_ref, out_ref)


def field_in_kernel(
    x_ref,
    own_ref,
    one_ref,
    other_ref,
    table_ref,
    half_ref,
    far_ref,
    turn_ref,
    out_ref,
    sems,
):
    copies = [pltpu.make_async_copy(half_ref, far_ref.at[:, 0:32, :], sems.at[4])]
    copies[0].start()
    me = lax.axis_index("beam")
    for step, ref in enumerate((own_ref, one_ref, other_ref.at[0], other_ref.at[1])):
        turn_ref[0, me ^ step] = jnp.cos(ref[...])
        turn_ref[1, me ^ step] = jnp.sin(ref[...])
    parts = []
    for m in range(4):
        cut = pl.ds(256 * m, 256)
        ur, ui = x_ref[0, :, cut].astype(f32), x_ref[1, :, cut].astype(f32)
        c, s = over_beams(turn_ref[0, m]), over_beams(turn_ref[1, m])
        wr, wi = ur * c - ui * s, ur * s + ui * c
        parts.append((wr.astype(bf16).astype(f32), wi.astype(bf16).astype(f32)))

    def ready(rho):
        place = pl.ds(16 * rho, 16)
        copy = pltpu.make_async_copy(
            out_ref.at[place], far_ref.at[place, 32:64, :], sems.at[rho]
        )
        copy.start()
        copies.append(copy)

    cols_in(parts, table_ref, out_ref, ready)
    for copy in copies:
        copy.wait()


def turned(pair, part, sign):
    if part == 0:
        return pair
    c = math.cos(2.0 * math.pi * part)
    s = sign * math.sin(2.0 * math.pi * part)
    return pair[0] * c - pair[1] * s, pair[0] * s + pair[1] * c


def sixteen(x, sign):
    four = split_four if sign < 0 else join_four
    low = [four([x[i + 4 * j] for j in range(4)]) for i in range(4)]
    out = [None] * 16
    for k in range(4):
        for j, pair in enumerate(four([turned(low[i][k], i * k / 16, sign) for i in range(4)])):
            out[k + 4 * j] = pair
    return out


def stacked(pairs):
    return [jnp.concatenate([pair[p] for pair in pairs], 0) for p in (0, 1)]


def rows_pass(v_ref, first, lanes, twist, h_ref, sign):
    quads = []
    for s1 in range(16):
        parts = []
        for m in range(4):
            s = 16 * m + s1
            parts.append(
                (
                    v_ref[s, first : first + 16, :].astype(f32),
                    v_ref[s, first + 16 : first + 32, :].astype(f32),
                )
            )
        quads.append(split_four(parts))
    done = []
    for sigma in range(4):
        got = sixteen([turned(quads[s1][sigma], sigma * s1 / 64, -1) for s1 in range(16)], -1)
        spun = []
        for q in range(16):
            tc, ts = twist[0, sigma, q : q + 1, :], twist[1, sigma, q : q + 1, :]
            ar, ai = got[q]
            spun.append(((ar * tc + ai * ts).astype(bf16), (ai * tc - ar * ts).astype(bf16)))
        spec = dot(jnp.concatenate(stacked(spun), 1), lanes[0])
        dr, di = spec[:, :128], spec[:, 128:]
        hc, hs = h_ref[0, sigma], h_ref[1, sigma]
        if sign > 0:
            er, ei = dr * hc - di * hs, dr * hs + di * hc
        else:
            er, ei = dr * hc + di * hs, di * hc - dr * hs
        back = dot(jnp.concatenate([er.astype(bf16), ei.astype(bf16)], 1), lanes[1])
        spun = []
        for q in range(16):
            tc, ts = twist[0, sigma, q : q + 1, :], twist[1, sigma, q : q + 1, :]
            gr, gi = back[16 * q : 16 * q + 16, :128], back[16 * q : 16 * q + 16, 128:]
            spun.append((gr * tc - gi * ts, gi * tc + gr * ts))
        got = sixteen(spun, 1)
        done.append([turned(got[s1], sigma * s1 / 64, 1) for s1 in range(16)])
    return [join_four([done[sigma][s1] for sigma in range(4)]) for s1 in range(16)]


def rows_kernel(v_ref, lanes, twist, h_ref, far_ref, pairs, sems):
    out_ref = pairs.reshape(64, 66, 128)
    copies = []
    for first, sign in ((0, -1), (32, 1)):
        done = rows_pass(v_ref, first, lanes, twist, h_ref, sign)
        for s1 in range(16):
            for m in range(4):
                for p in (0, 1):
                    out_ref[16 * m + s1, first + 16 * p : first + 16 * p + 16, :] = (
                        done[s1][m][p].astype(bf16)
                    )
        if not first:
            copies.append(
                pltpu.make_async_copy(pairs.at[:, 0:16], far_ref.at[:, 0:16], sems.at[0])
            )
            copies[0].start()
    sum_re = jnp.zeros((16, 128), f32)
    sum_im = jnp.zeros((16, 128), f32)
    for s1 in range(16):
        for m in range(4):
            fr, fi = done[s1][m]
            tr = v_ref[16 * m + s1, 0:16, :].astype(f32)
            ti = v_ref[16 * m + s1, 16:32, :].astype(f32)
            sum_re = sum_re + (tr * fr + ti * fi)
            sum_im = sum_im + (tr * fi - ti * fr)
    re = jnp.sum(sum_re, 0, keepdims=True)
    im = jnp.sum(sum_im, 0, keepdims=True)
    both = jnp.concatenate([re, im], 0)
    both = both + pltpu.roll(both, 64, 1)
    high = both.astype(bf16).astype(f32)
    lane = lax.broadcasted_iota(jnp.int32, (2, 128), 1)
    tail = jnp.where(lane < 64, high, both - high).astype(bf16)
    out_ref[:, 64:66, :] = jnp.broadcast_to(tail[None], (64, 2, 128))
    copies.append(pltpu.make_async_copy(pairs.at[:, 16:33], far_ref.at[:, 16:33], sems.at[1]))
    copies[1].start()
    for copy in copies:
        copy.wait()


def cols_out(pairs_ref, first, table_ref):
    v_ref = pairs_ref.reshape(64, 66, 128)
    done = []
    for rho in range(4):
        cut = pl.ds(16 * rho, 16)
        both = jnp.concatenate(
            [
                v_ref[cut, first : first + 16, :].reshape(256, 128),
                v_ref[cut, first + 16 : first + 32, :].reshape(256, 128),
            ],
            1,
        )
        prod = dot(both, table_ref[rho if rho < 3 else 1], ((0,), (0,)))
        sign = -1 if rho == 3 else 1
        done.append(
            (
                prod[:128, :256] - sign * prod[128:, 256:],
                prod[128:, :256] + sign * prod[:128, 256:],
            )
        )
    return join_four(done)


def beam_sums(pairs_ref):
    rows = jnp.sum(pairs_ref[:, 32, :, :].astype(f32), 0)
    lane = lax.broadcasted_iota(jnp.int32, (8, 128), 1) % 8
    beam = lax.broadcasted_iota(jnp.int32, (8, 128), 0)
    sums = []
    for p in (0, 1):
        line = rows[p : p + 1] / N
        picked = jnp.where(lane == beam, jnp.broadcast_to(line, (8, 128)), 0.0)
        sums.append(jnp.sum(picked, 1, keepdims=True))
    return sums


def target_out_kernel(
    v_ref,
    x_ref,
    turn_ref,
    table_ref,
    back_ref,
    over_ref,
    keep_ref,
    near_ref,
    whole,
):
    sums = beam_sums(v_ref)
    lanes = lax.broadcasted_iota(jnp.int32, (8, 8), 1)
    beams = lax.broadcasted_iota(jnp.int32, (8, 8), 0)
    for p in (0, 1):
        over_ref[p : p + 1, :] = jnp.sum(jnp.where(lanes == beams, sums[p], 0.0), 0, keepdims=True)
    for m, (ar, ai) in enumerate(cols_out(v_ref, 0, table_ref)):
        cut = pl.ds(256 * m, 256)
        c, s = over_beams(turn_ref[0, m]), over_beams(turn_ref[1, m])
        br, bi = ar * c + ai * s, ai * c - ar * s
        back_ref[0, :, cut] = br.astype(bf16)
        back_ref[1, :, cut] = bi.astype(bf16)
        ur, ui = x_ref[0, :, cut].astype(f32), x_ref[1, :, cut].astype(f32)
        zr = (br * ur + bi * ui).reshape(16, 8, 256)
        zi = (br * ui - bi * ur).reshape(16, 8, 256)
        whole[m] = -(2.0 / BEAMS) * jnp.sum(sums[0][None] * zi - sums[1][None] * zr, 1)
    me = lax.axis_index("beam")
    for place, step in enumerate((0, 2)):
        keep_ref[place] = whole[me ^ step]
        near_ref[place] = whole[me ^ step ^ 1]


def field_out_kernel(v_ref, table_ref, held_ref, out_ref, back_ref):
    back_ref[...] = held_ref[...]
    for m, (ar, ai) in enumerate(cols_out(v_ref, 32, table_ref)):
        cut = pl.ds(256 * m, 256)
        out_ref[0, :, cut] = ar.astype(bf16)
        out_ref[1, :, cut] = ai.astype(bf16)


def call(kernel, name, outs, args, flops, scratch=(), far=()):
    in_vmem = pl.BlockSpec(memory_space=pltpu.VMEM)
    in_hbm = pl.BlockSpec(memory_space=pltpu.HBM)
    many = isinstance(outs, tuple)
    specs = tuple(in_hbm if i in far else in_vmem for i in range(len(outs) if many else 1))
    size = sum(a.size * a.dtype.itemsize for a in args)
    return pl.pallas_call(
        kernel,
        name=name,
        out_shape=outs,
        in_specs=[in_vmem] * len(args),
        out_specs=specs if many else specs[0],
        scratch_shapes=list(scratch),
        compiler_params=pltpu.CompilerParams(vmem_limit_bytes=VMEM_LIMIT),
        cost_estimate=pl.CostEstimate(flops=flops, bytes_accessed=size, transcendentals=0),
    )(*args)


def shape(dims, dtype):
    return jax.ShapeDtypeStruct(dims, dtype)


FLOPS = 4 * 2 * 512 * 256 * 256


def local(field_in, target, phase, moment, second):
    tab = {name: jnp.asarray(value) for name, value in host_tables().items()}
    field = field_in.reshape(2, 128, N)
    goal = target.reshape(2, 128, N)

    def swap(x):
        return lax.all_to_all(x, "row", split_axis=0, concat_axis=0, tiled=True)

    def trade(x, step):
        return lax.ppermute(x, "beam", [(i, i ^ step) for i in range(4)])

    plane = shape((2, 128, N), bf16)
    pieces = shape((2, 16, 256), f32)
    one = trade(phase, 1)
    phases = (phase, one, trade(jnp.stack([phase, one]), 2))
    half = call(
        target_in_kernel,
        "target_in",
        shape((64, 32, 128), bf16),
        (goal, tab["col_left"]),
        FLOPS,
    )
    cols, turn = call(
        field_in_kernel,
        "field_in",
        (shape((64, 64, 128), bf16), shape((2, 4, 16, 256), f32)),
        (field,) + phases + (tab["col_left"], half),
        FLOPS,
        (pltpu.VMEM((64, 32, 128), bf16), pltpu.SemaphoreType.DMA((5,))),
        (0,),
    )
    cols = swap(cols)
    h = transfer(lax.axis_index("row"))
    spread = call(
        rows_kernel,
        "rows",
        shape((64, 33, 2, 128), bf16),
        (cols, tab["lanes"], tab["twist"], h),
        6 * FLOPS,
        (pltpu.VMEM((64, 33, 2, 128), bf16), pltpu.SemaphoreType.DMA((2,))),
        (0,),
    )
    spread = swap(spread)
    held, over, keep, near = call(
        target_out_kernel,
        "target_out",
        (plane, shape((2, 8), f32), pieces, pieces),
        (spread, field, turn, tab["col_right"]),
        FLOPS,
        (pltpu.VMEM((4, 16, 256), f32),),
    )
    mine = keep + trade(near, 1)
    grad = mine[0] + trade(mine[1], 2)
    forward, back = call(
        field_out_kernel,
        "field_out",
        (plane, plane),
        (spread, tab["col_right"], held),
        FLOPS,
    )
    new_moment = 0.9 * moment + 0.1 * grad
    new_second = 0.999 * second + 0.001 * grad * grad
    corr_one = 1.0 - 0.9**STEP
    corr_two = 1.0 - 0.999**STEP
    new_phase = phase - learn_rate * (new_moment / corr_one) / (
        jnp.sqrt(new_second / corr_two) + 1e-08
    )
    split = (2, 16, 8, N)
    return (forward.reshape(split), back.reshape(split), over, new_phase, new_moment, new_second)


def solution(mesh):
    return jax.shard_map(
        local,
        mesh=mesh,
        in_specs=(
            P(None, "row", "beam", None),
            P(None, "row", "beam", None),
            P("row", "beam"),
            P("row", "beam"),
            P("row", "beam"),
        ),
        out_specs=(
            P(None, "row", "beam", None),
            P(None, "row", "beam", None),
            P(None, "beam"),
            P("row", "beam"),
            P("row", "beam"),
            P("row", "beam"),
        ),
        check_vma=False,
    )
```

```python
import functools
import math

import jax
import jax.numpy as jnp
import ml_dtypes
import numpy as np
from jax import lax
from jax.experimental import pallas as pl
from jax.experimental.pallas import tpu as pltpu
from jax.sharding import PartitionSpec as P


STEP = 10
N = 1024
BEAMS = 32
learn_rate = 0.4
f32 = jnp.float32
bf16 = jnp.bfloat16
VMEM_LIMIT = 48 * 1024 * 1024


def angles(product, size):
    turn = (product % size) * (2.0 * math.pi / size)
    return np.cos(turn), np.sin(turn)


def as_bf16(array):
    return array.astype(np.float32).astype(ml_dtypes.bfloat16)


LIFT = 1.1328125
FITTED = 1.13280406


@functools.lru_cache(None)
def host_tables():
    k = np.arange(256)
    left, right = [], []
    for rho in range(3):
        c, s = angles((4 * k[:, None] + rho) * k[None, :], 1024)
        left.append(np.concatenate([c, s], 0) / 32.0)
        right.append(np.concatenate([c, s], 1) / 32.0)
    q = np.arange(16)
    c, s = angles(q[:, None] * q[None, :], 16)
    kc, ks = np.kron(c * LIFT, np.eye(8)), np.kron(s * LIFT, np.eye(8))
    lane_in = np.block([[kc, -ks], [ks, kc]])
    lane_out = np.block([[kc, ks], [-ks, kc]])
    k1 = 4 * q[None, :, None] + np.arange(4)[:, None, None]
    r = np.repeat(q, 8)[None, None, :]
    twist = np.stack(angles(k1 * r, 1024)).astype(np.float32)
    return dict(
        col_left=as_bf16(np.stack(left)),
        col_right=as_bf16(np.stack(right)),
        lanes=as_bf16(np.stack([lane_in, lane_out])),
        twist=twist,
    )


def frequency(index):
    return jnp.where(index < N // 2, index, index - N).astype(f32)


def transfer(row_index):
    rho, a = row_index // 16, row_index % 16
    shape = (4, 16, 16, 128)
    sigma = lax.broadcasted_iota(jnp.int32, shape, 0)
    q = lax.broadcasted_iota(jnp.int32, shape, 1)
    t = lax.broadcasted_iota(jnp.int32, shape, 2)
    k2 = lax.broadcasted_iota(jnp.int32, shape, 3) // 8
    fy = frequency(4 * q + sigma + 64 * k2)
    k = 4 * (16 * a + t)
    fx = frequency(jnp.where(rho == 3, 1023 - k, k + rho))
    half = float(N // 2)
    rad = (fy**2 + fx**2) / (half * half)
    theta = -60.0 * rad / (1.0 + jnp.sqrt(1.0 - 0.4 * rad))
    scale = 1.0 / (N * FITTED * FITTED)
    return jnp.stack([jnp.cos(theta) * scale, jnp.sin(theta) * scale]).reshape(2, 4, 256, 128)


def split_four(x):
    e0 = [x[0][p] + x[2][p] for p in (0, 1)]
    e1 = [x[0][p] - x[2][p] for p in (0, 1)]
    o0 = [x[1][p] + x[3][p] for p in (0, 1)]
    o1 = [x[1][p] - x[3][p] for p in (0, 1)]
    return (
        (e0[0] + o0[0], e0[1] + o0[1]),
        (e1[0] + o1[1], e1[1] - o1[0]),
        (e0[0] - o0[0], e0[1] - o0[1]),
        (e1[0] - o1[1], e1[1] + o1[0]),
    )


def join_four(x):
    e0 = [x[0][p] + x[2][p] for p in (0, 1)]
    e1 = [x[0][p] - x[2][p] for p in (0, 1)]
    o0 = [x[1][p] + x[3][p] for p in (0, 1)]
    o1 = [x[1][p] - x[3][p] for p in (0, 1)]
    return (
        (e0[0] + o0[0], e0[1] + o0[1]),
        (e1[0] - o1[1], e1[1] + o1[0]),
        (e0[0] - o0[0], e0[1] - o0[1]),
        (e1[0] + o1[1], e1[1] - o1[0]),
    )


def dot(a, b, dims=((1,), (0,))):
    return lax.dot_general(a, b, (dims, ((), ())), preferred_element_type=f32)


def over_beams(rows):
    return jnp.broadcast_to(rows[:, None, :], (16, 8, rows.shape[1])).reshape(128, rows.shape[1])


def two_bf16(x):
    high = x.astype(bf16)
    return high, (x - high.astype(f32)).astype(bf16)


def cols_in(parts, table_ref, out_ref, ready=lambda rho: None):
    for rho, (ur, ui) in enumerate(split_four(parts)):
        high, low = two_bf16(jnp.concatenate([ur, ui], 0))
        left = table_ref[rho if rho < 3 else 1]
        prod = dot(left, high, ((1,), (1,))) + dot(left, low, ((1,), (1,)))
        sign = -1 if rho == 3 else 1
        yr = prod[:256, :128] + sign * prod[256:, 128:]
        yi = prod[:256, 128:] - sign * prod[256:, :128]
        place = slice(16 * rho, 16 * rho + 16)
        out_ref[place, 0:16, :] = yr.astype(bf16).reshape(16, 16, 128)
        out_ref[place, 16:32, :] = yi.astype(bf16).reshape(16, 16, 128)
        ready(rho)


def target_in_kernel(x_ref, table_ref, out_ref):
    parts = []
    for m in range(4):
        cut = pl.ds(256 * m, 256)
        parts.append((x_ref[0, :, cut].astype(f32), x_ref[1, :, cut].astype(f32)))
    cols_in(parts, table_ref, out_ref)


def field_in_kernel(
    x_ref,
    own_ref,
    one_ref,
    other_ref,
    table_ref,
    half_ref,
    far_ref,
    turn_ref,
    out_ref,
    sems,
):
    copies = [pltpu.make_async_copy(half_ref, far_ref.at[:, 0:32, :], sems.at[4])]
    copies[0].start()
    me = lax.axis_index("beam")
    for step, ref in enumerate((own_ref, one_ref, other_ref.at[0], other_ref.at[1])):
        turn_ref[0, me ^ step] = jnp.cos(ref[...])
        turn_ref[1, me ^ step] = jnp.sin(ref[...])
    parts = []
    for m in range(4):
        cut = pl.ds(256 * m, 256)
        ur, ui = x_ref[0, :, cut].astype(f32), x_ref[1, :, cut].astype(f32)
        c, s = over_beams(turn_ref[0, m]), over_beams(turn_ref[1, m])
        wr, wi = ur * c - ui * s, ur * s + ui * c
        parts.append((wr.astype(bf16).astype(f32), wi.astype(bf16).astype(f32)))

    def ready(rho):
        place = pl.ds(16 * rho, 16)
        copy = pltpu.make_async_copy(
            out_ref.at[place], far_ref.at[place, 32:64, :], sems.at[rho]
        )
        copy.start()
        copies.append(copy)

    cols_in(parts, table_ref, out_ref, ready)
    for copy in copies:
        copy.wait()


def turned(pair, part, sign):
    if part == 0:
        return pair
    c = math.cos(2.0 * math.pi * part)
    s = sign * math.sin(2.0 * math.pi * part)
    return pair[0] * c - pair[1] * s, pair[0] * s + pair[1] * c


def sixteen(x, sign):
    four = split_four if sign < 0 else join_four
    low = [four([x[i + 4 * j] for j in range(4)]) for i in range(4)]
    out = [None] * 16
    for k in range(4):
        for j, pair in enumerate(four([turned(low[i][k], i * k / 16, sign) for i in range(4)])):
            out[k + 4 * j] = pair
    return out


def stacked(pairs):
    return [jnp.concatenate([pair[p] for pair in pairs], 0) for p in (0, 1)]


def rows_pass(v_ref, first, lanes, twist, h_ref, sign):
    quads = []
    for s1 in range(16):
        parts = []
        for m in range(4):
            s = 16 * m + s1
            parts.append(
                (
                    v_ref[s, first : first + 16, :].astype(f32),
                    v_ref[s, first + 16 : first + 32, :].astype(f32),
                )
            )
        quads.append(split_four(parts))
    done = []
    for sigma in range(4):
        got = sixteen([turned(quads[s1][sigma], sigma * s1 / 64, -1) for s1 in range(16)], -1)
        spun = []
        for q in range(16):
            tc, ts = twist[0, sigma, q : q + 1, :], twist[1, sigma, q : q + 1, :]
            ar, ai = got[q]
            spun.append(((ar * tc + ai * ts).astype(bf16), (ai * tc - ar * ts).astype(bf16)))
        spec = dot(jnp.concatenate(stacked(spun), 1), lanes[0])
        dr, di = spec[:, :128], spec[:, 128:]
        hc, hs = h_ref[0, sigma], h_ref[1, sigma]
        if sign > 0:
            er, ei = dr * hc - di * hs, dr * hs + di * hc
        else:
            er, ei = dr * hc + di * hs, di * hc - dr * hs
        back = dot(jnp.concatenate([er.astype(bf16), ei.astype(bf16)], 1), lanes[1])
        spun = []
        for q in range(16):
            tc, ts = twist[0, sigma, q : q + 1, :], twist[1, sigma, q : q + 1, :]
            gr, gi = back[16 * q : 16 * q + 16, :128], back[16 * q : 16 * q + 16, 128:]
            spun.append((gr * tc - gi * ts, gi * tc + gr * ts))
        got = sixteen(spun, 1)
        done.append([turned(got[s1], sigma * s1 / 64, 1) for s1 in range(16)])
    return [join_four([done[sigma][s1] for sigma in range(4)]) for s1 in range(16)]


def rows_kernel(v_ref, lanes, twist, h_ref, far_ref, out_ref, tail_ref, sems):
    far_rows = far_ref.reshape(64, 66, 128)
    copies = []
    for first, sign in ((0, -1), (32, 1)):
        done = rows_pass(v_ref, first, lanes, twist, h_ref, sign)
        for s1 in range(16):
            for m in range(4):
                for p in (0, 1):
                    out_ref[16 * m + s1, first + 16 * p : first + 16 * p + 16, :] = (
                        done[s1][m][p].astype(bf16)
                    )
        if not first:
            copies.append(
                pltpu.make_async_copy(out_ref.at[:, 0:32], far_rows.at[:, 0:32], sems.at[0])
            )
            copies[0].start()
    sum_re = jnp.zeros((16, 128), f32)
    sum_im = jnp.zeros((16, 128), f32)
    for s1 in range(16):
        for m in range(4):
            fr, fi = done[s1][m]
            tr = v_ref[16 * m + s1, 0:16, :].astype(f32)
            ti = v_ref[16 * m + s1, 16:32, :].astype(f32)
            sum_re = sum_re + (tr * fr + ti * fi)
            sum_im = sum_im + (tr * fi - ti * fr)
    re = jnp.sum(sum_re, 0, keepdims=True)
    im = jnp.sum(sum_im, 0, keepdims=True)
    both = jnp.concatenate([re, im], 0)
    both = both + pltpu.roll(both, 64, 1)
    high = both.astype(bf16).astype(f32)
    lane = lax.broadcasted_iota(jnp.int32, (2, 128), 1)
    tail = jnp.where(lane < 64, high, both - high).astype(bf16)
    tail_ref[...] = jnp.broadcast_to(tail[None], (64, 2, 128))
    copies.append(pltpu.make_async_copy(out_ref.at[:, 32:64], far_rows.at[:, 32:64], sems.at[1]))
    copies.append(pltpu.make_async_copy(tail_ref, far_ref.at[:, 32], sems.at[2]))
    copies[1].start()
    copies[2].start()
    for copy in copies:
        copy.wait()


def cols_out(pairs_ref, first, table_ref):
    v_ref = pairs_ref.reshape(64, 66, 128)
    done = []
    for rho in range(4):
        cut = pl.ds(16 * rho, 16)
        both = jnp.concatenate(
            [
                v_ref[cut, first : first + 16, :].reshape(256, 128),
                v_ref[cut, first + 16 : first + 32, :].reshape(256, 128),
            ],
            1,
        )
        prod = dot(both, table_ref[rho if rho < 3 else 1], ((0,), (0,)))
        sign = -1 if rho == 3 else 1
        done.append(
            (
                prod[:128, :256] - sign * prod[128:, 256:],
                prod[128:, :256] + sign * prod[:128, 256:],
            )
        )
    return join_four(done)


def beam_sums(pairs_ref):
    rows = jnp.sum(pairs_ref[:, 32, :, :].astype(f32), 0)
    lane = lax.broadcasted_iota(jnp.int32, (8, 128), 1) % 8
    beam = lax.broadcasted_iota(jnp.int32, (8, 128), 0)
    sums = []
    for p in (0, 1):
        line = rows[p : p + 1] / N
        picked = jnp.where(lane == beam, jnp.broadcast_to(line, (8, 128)), 0.0)
        sums.append(jnp.sum(picked, 1, keepdims=True))
    return sums


def target_out_kernel(
    v_ref,
    x_ref,
    turn_ref,
    table_ref,
    back_ref,
    over_ref,
    keep_ref,
    near_ref,
    whole,
):
    sums = beam_sums(v_ref)
    lanes = lax.broadcasted_iota(jnp.int32, (8, 8), 1)
    beams = lax.broadcasted_iota(jnp.int32, (8, 8), 0)
    for p in (0, 1):
        over_ref[p : p + 1, :] = jnp.sum(jnp.where(lanes == beams, sums[p], 0.0), 0, keepdims=True)
    for m, (ar, ai) in enumerate(cols_out(v_ref, 0, table_ref)):
        cut = pl.ds(256 * m, 256)
        c, s = over_beams(turn_ref[0, m]), over_beams(turn_ref[1, m])
        br, bi = ar * c + ai * s, ai * c - ar * s
        back_ref[0, :, cut] = br.astype(bf16)
        back_ref[1, :, cut] = bi.astype(bf16)
        ur, ui = x_ref[0, :, cut].astype(f32), x_ref[1, :, cut].astype(f32)
        zr = (br * ur + bi * ui).reshape(16, 8, 256)
        zi = (br * ui - bi * ur).reshape(16, 8, 256)
        whole[m] = -(2.0 / BEAMS) * jnp.sum(sums[0][None] * zi - sums[1][None] * zr, 1)
    me = lax.axis_index("beam")
    for place, step in enumerate((0, 2)):
        keep_ref[place] = whole[me ^ step]
        near_ref[place] = whole[me ^ step ^ 1]


def field_out_kernel(v_ref, table_ref, held_ref, out_ref, back_ref):
    back_ref[...] = held_ref[...]
    for m, (ar, ai) in enumerate(cols_out(v_ref, 32, table_ref)):
        cut = pl.ds(256 * m, 256)
        out_ref[0, :, cut] = ar.astype(bf16)
        out_ref[1, :, cut] = ai.astype(bf16)


def call(kernel, name, outs, args, flops, scratch=(), far=()):
    in_vmem = pl.BlockSpec(memory_space=pltpu.VMEM)
    in_hbm = pl.BlockSpec(memory_space=pltpu.HBM)
    many = isinstance(outs, tuple)
    specs = tuple(in_hbm if i in far else in_vmem for i in range(len(outs) if many else 1))
    size = sum(a.size * a.dtype.itemsize for a in args)
    return pl.pallas_call(
        kernel,
        name=name,
        out_shape=outs,
        in_specs=[in_vmem] * len(args),
        out_specs=specs if many else specs[0],
        scratch_shapes=list(scratch),
        compiler_params=pltpu.CompilerParams(vmem_limit_bytes=VMEM_LIMIT),
        cost_estimate=pl.CostEstimate(flops=flops, bytes_accessed=size, transcendentals=0),
    )(*args)


def shape(dims, dtype):
    return jax.ShapeDtypeStruct(dims, dtype)


FLOPS = 4 * 2 * 512 * 256 * 256


def local(field_in, target, phase, moment, second):
    tab = {name: jnp.asarray(value) for name, value in host_tables().items()}
    field = field_in.reshape(2, 128, N)
    goal = target.reshape(2, 128, N)

    def swap(x):
        return lax.all_to_all(x, "row", split_axis=0, concat_axis=0, tiled=True)

    def trade(x, step):
        return lax.ppermute(x, "beam", [(i, i ^ step) for i in range(4)])

    plane = shape((2, 128, N), bf16)
    pieces = shape((2, 16, 256), f32)
    one = trade(phase, 1)
    phases = (phase, one, trade(jnp.stack([phase, one]), 2))
    half = call(
        target_in_kernel,
        "target_in",
        shape((64, 32, 128), bf16),
        (goal, tab["col_left"]),
        FLOPS,
    )
    cols, turn = call(
        field_in_kernel,
        "field_in",
        (shape((64, 64, 128), bf16), shape((2, 4, 16, 256), f32)),
        (field,) + phases + (tab["col_left"], half),
        FLOPS,
        (pltpu.VMEM((64, 32, 128), bf16), pltpu.SemaphoreType.DMA((5,))),
        (0,),
    )
    cols = swap(cols)
    h = transfer(lax.axis_index("row"))
    spread = call(
        rows_kernel,
        "rows",
        shape((64, 33, 2, 128), bf16),
        (cols, tab["lanes"], tab["twist"], h),
        6 * FLOPS,
        (
            pltpu.VMEM((64, 64, 128), bf16),
            pltpu.VMEM((64, 2, 128), bf16),
            pltpu.SemaphoreType.DMA((3,)),
        ),
        (0,),
    )
    spread = swap(spread)
    held, over, keep, near = call(
        target_out_kernel,
        "target_out",
        (plane, shape((2, 8), f32), pieces, pieces),
        (spread, field, turn, tab["col_right"]),
        FLOPS,
        (pltpu.VMEM((4, 16, 256), f32),),
    )
    mine = keep + trade(near, 1)
    grad = mine[0] + trade(mine[1], 2)
    forward, back = call(
        field_out_kernel,
        "field_out",
        (plane, plane),
        (spread, tab["col_right"], held),
        FLOPS,
    )
    new_moment = 0.9 * moment + 0.1 * grad
    new_second = 0.999 * second + 0.001 * grad * grad
    corr_one = 1.0 - 0.9**STEP
    corr_two = 1.0 - 0.999**STEP
    new_phase = phase - learn_rate * (new_moment / corr_one) / (
        jnp.sqrt(new_second / corr_two) + 1e-08
    )
    split = (2, 16, 8, N)
    return (forward.reshape(split), back.reshape(split), over, new_phase, new_moment, new_second)


def solution(mesh):
    return jax.shard_map(
        local,
        mesh=mesh,
        in_specs=(
            P(None, "row", "beam", None),
            P(None, "row", "beam", None),
            P("row", "beam"),
            P("row", "beam"),
            P("row", "beam"),
        ),
        out_specs=(
            P(None, "row", "beam", None),
            P(None, "row", "beam", None),
            P(None, "beam"),
            P("row", "beam"),
            P("row", "beam"),
            P("row", "beam"),
        ),
        check_vma=False,
    )
```
